128 devices in a mesh: section: 16 (over z, x), dp: 8 (over y, core).
Axes of the slice: x: 4, y: 4, z: 4, core: 2. Of those that a mesh axis runs over, the one named last changes fastest.
Arguments:
- cotangent: bfloat16 [4, 128, 6144], P(None, 'dp'), may hold values from -6 to 6
- saved_inputs: bfloat16 [2, 16, 4, 128, 6144], P(None, 'section', None, 'dp'), may hold values from -6 to 6
- weights: bfloat16 [2, 16, 3072, 6144], P(None, 'section', 'dp'), may hold values from -0.0546875 to 0.0546875
Outputs:
- section_grads: bfloat16 [16, 4, 128, 6144], P('section', None, 'dp')
- weight_grads: bfloat16 [2, 16, 3072, 6144], P(None, 'section', 'dp')
- grad_peak: float32 [], replicated
The draws below stay inside these ranges and needn't reach their ends.
All inputs are finite; a program needn't handle non-finite values.
Results may differ from the reference program's by a relative error of at most 0.039.
Values may be sent and summed in bfloat16 or wider, within the bound.
A program may use at most 128 MiB of HBM per device.

```python
import jax
import jax.numpy as jnp
from jax import lax

D = 6144
H = 3072
MB = 4
TOKENS = 128
N_SECTION = 16


def level_of(stream_key, shape, pieces, least, high):
    level, own = 1.0, jax.random.fold_in(stream_key, 6)
    for dim, blocks in pieces:
        steps = jnp.exp(jax.random.uniform(jax.random.fold_in(own, dim), (blocks,), jnp.float32, least / len(pieces), high / len(pieces)))
        level = level * jnp.repeat(steps, shape[dim] // blocks).reshape([-1 if axis == dim else 1 for axis in range(len(shape))])
    return level


def scatter_about(own_key, shape, deviation, most, pieces=(), held_as=jnp.bfloat16):
    array = deviation * jax.random.normal(own_key, shape, jnp.float32)
    if pieces:
        array = array * level_of(own_key, shape, pieces, -0.22, 0.18)
    return jnp.clip(array, -most, most).astype(held_as)


def setup_inputs(seed: int = 0) -> dict:
    key_list = jax.random.split(jax.random.key(seed), 4)
    return {
        "cotangent": scatter_about(key_list[0], (MB, TOKENS, D), 1.0, 6.0, ((1, 8),)),
        "saved_inputs": scatter_about(key_list[1], (2, N_SECTION, MB, TOKENS, D), 1.0, 6.0, ((1, 16), (3, 8))),
        "weights": scatter_about(key_list[2], (2, N_SECTION, H, D), (2 * D) ** -0.5, 0.0546875, ((1, 16), (2, 8))),
    }


epsilon = 1e-05

def norm_parts(inputs):
    values = inputs.astype(jnp.float32)
    scale = lax.rsqrt(lax.optimization_barrier(jnp.mean(values * values, axis=-1, keepdims=True)) + epsilon)
    normed = values * scale
    half = normed.shape[-1] // 2
    first = normed[..., :half]
    gated = jax.nn.sigmoid(normed[..., half:])
    return (normed, scale, first, gated)

def input_grad(cot_in, inputs, head_grad):
    normed, scale, first, gated = norm_parts(inputs)
    norm_grad = jnp.concatenate([head_grad * gated, head_grad * first * gated * (1.0 - gated)], axis=-1)
    result = cot_in.astype(jnp.float32) + scale * (norm_grad - normed * lax.optimization_barrier(jnp.mean(norm_grad * normed, axis=-1, keepdims=True)))
    return result.astype(jnp.bfloat16)

def features(inputs):
    normed, scale, first, gated = norm_parts(inputs)
    return (first * gated).astype(jnp.bfloat16)

def reference(cotangent, saved_inputs, weights):
    sections = N_SECTION
    width = cotangent.shape[-1]
    flowing = cotangent.reshape(-1, width)
    visited = []
    leaving = []
    for step_index in range(2 * sections):
        virtual = 2 * sections - 1 - step_index
        if virtual >= sections:
            side = 1
            holder = 2 * sections - 1 - virtual
        else:
            side = 0
            holder = virtual
        inputs = saved_inputs[side, holder].reshape(-1, width)
        rows = weights[side, holder]
        head_grad = lax.dot_general(flowing, rows, (((1,), (1,)), ((), ())), preferred_element_type=jnp.float32)
        visited.append((side, holder, flowing, inputs))
        flowing = input_grad(flowing, inputs, head_grad)
        if side == 0:
            leaving.append((holder, flowing.reshape(cotangent.shape)))
    leaving.sort(key=lambda pair: pair[0])
    section_grads = jnp.stack([pair[1] for pair in leaving], axis=0)
    total = jnp.zeros((), jnp.float32)
    largest = jnp.zeros((), jnp.float32)
    for side, holder, cot_in, inputs in visited:
        grad = lax.dot_general(features(inputs), cot_in, (((0,), (0,)), ((), ())), preferred_element_type=jnp.float32)
        total = total + jnp.sum(grad * grad)
        largest = jnp.maximum(largest, jnp.max(jnp.abs(grad)))
    limit = 0.5 * jnp.sqrt(jnp.float32(2 * sections * (width // 2) * width))
    factor = jnp.minimum(jnp.float32(1.0), limit / jnp.sqrt(total))
    slots = [[None] * sections, [None] * sections]
    for side, holder, cot_in, inputs in visited:
        grad = lax.dot_general(features(inputs), cot_in, (((0,), (0,)), ((), ())), preferred_element_type=jnp.float32)
        slots[side][holder] = (grad * factor).astype(jnp.bfloat16)
    weight_grads = jnp.stack([jnp.stack(slots[0], axis=0), jnp.stack(slots[1], axis=0)], axis=0)
    return (section_grads, weight_grads, factor * largest)
```

```python
import functools

import jax
import jax.numpy as jnp
from jax import lax
from jax.experimental import pallas as pl
from jax.experimental.pallas import tpu as pltpu
from jax.sharding import PartitionSpec as P

epsilon = 1e-05
MESH = pl.DeviceIdType.MESH
T = 32
LAG = (3, 5)


def relay_kernel(
    ns, nb, hs, nc, wt_hbm, xp_hbm, cot_hbm, coef, h_t, x_own,
    grads, leaving, stats,
    wt, xg, u, q, sbuf, obuf, gtile, stat_dp, stat_sec, stat_me,
    recv, relay_sem, send_sem, own_send, own_recv, load_sem, tile_sem, stat_send, stat_recv,
):
    f32 = jnp.float32
    s = lax.axis_index("section")
    me = lax.axis_index("dp")
    y = lax.div(me, 2)
    c = lax.rem(me, 2)
    ny = nb // 2
    partner = me + 1 - 2 * c
    per_owner = nc // nb
    wide = 2 * hs + 128

    loads = []
    for leg in range(2):
        loads.append(pltpu.make_async_copy(wt_hbm.at[leg], wt.at[leg], load_sem.at[leg, 0]))
        loads.append(pltpu.make_async_copy(xp_hbm.at[leg], xg.at[leg], load_sem.at[leg, 1]))
    for copy in loads:
        copy.start()

    barrier = pltpu.get_barrier_semaphore()

    def greet(section, dp):
        pl.semaphore_signal(
            barrier, inc=1, device_id={"section": section, "dp": dp}, device_id_type=MESH
        )

    for j in range(1, nb):
        greet(s, lax.rem(me + j, nb))
    for j in range(1, ns):
        greet(lax.rem(s + j, ns), me)

    @pl.when(s < ns - 1)
    def _():
        for j in range(ny):
            greet(s + 1, 2 * j + c)

    @pl.when(s > 0)
    def _():
        for j in range(ny):
            greet(s - 1, 2 * j + c)

    pl.semaphore_wait(
        barrier, nb - 1 + ns - 1 + ny * jnp.where(s < ns - 1, 1, 0) + ny * jnp.where(s > 0, 1, 0)
    )

    @pl.when(s == 0)
    def _():
        copy = pltpu.make_async_copy(cot_hbm, u.at[0], load_sem.at[0, 2])
        copy.start()
        copy.wait()

    for copy in loads:
        copy.wait()

    for leg in range(2):
        def fill(k, _, leg=leg):
            total = jnp.zeros((T, hs), f32)
            for b in range(nb):
                total += jnp.dot(xg[leg, k, b], wt[leg, b], preferred_element_type=f32)
            q[leg, k] = total
            return 0

        lax.fori_loop(0, nc, fill, 0)

    def step(leg, k):
        first = (s == 0) if leg == 0 else False
        acc = jnp.zeros((T, hs), f32)

        def arrived(b):
            block = u.at[leg, k, b]
            pltpu.make_async_copy(block, block, recv.at[leg, k, b]).wait()

        for dy in (0, 1, 3, 2):
            b = 2 * lax.rem(y + dy, ny) + c

            def pass_on(b=b):
                arrived(b)
                pltpu.make_async_remote_copy(
                    src_ref=u.at[leg, k, b],
                    dst_ref=u.at[leg, k, b],
                    send_sem=relay_sem.at[leg, k],
                    recv_sem=recv.at[leg, k, b],
                    device_id={"section": s, "dp": partner},
                    device_id_type=MESH,
                ).start()

            if leg == 0:
                pl.when(s > 0)(pass_on)
            else:
                pass_on()
            acc += jnp.dot(u[leg, k, b][:, : 2 * hs], wt[leg, b], preferred_element_type=f32)
        for dy in (0, 1, 3, 2):
            b = 2 * lax.rem(y + dy, ny) + 1 - c
            if leg == 0:
                pl.when(s > 0)(functools.partial(arrived, b))
            else:
                arrived(b)
            acc += jnp.dot(u[leg, k, b][:, : 2 * hs], wt[leg, b], preferred_element_type=f32)
        kap = u[leg, k, 0][:, 2 * hs :].astype(f32)
        for b in range(1, nb):
            kap += u[leg, k, b][:, 2 * hs :].astype(f32)
        kap = jnp.concatenate([kap] * (hs // 128), axis=1)
        dh = acc - kap * q[leg, k]
        mine = u[leg, k, me].astype(f32)
        x_mine = xg[leg, k, me].astype(f32)
        new_a = mine[:, :hs] - kap * x_mine[:, :hs] + coef[leg, 0, k] * dh
        new_g = mine[:, hs : 2 * hs] - kap * x_mine[:, hs:] + coef[leg, 1, k] * dh
        part = jnp.sum(coef[leg, 2, k] * dh, axis=1, keepdims=True)
        sbuf[leg, k, :, :hs] = new_a.astype(jnp.bfloat16)
        sbuf[leg, k, :, hs : 2 * hs] = new_g.astype(jnp.bfloat16)
        sbuf[leg, k, :, 2 * hs :] = jnp.broadcast_to(part, (T, 128)).astype(jnp.bfloat16)

        def send(section, to_leg, dys):
            for dy in dys:
                pltpu.make_async_remote_copy(
                    src_ref=sbuf.at[leg, k],
                    dst_ref=u.at[to_leg, k, me],
                    send_sem=send_sem.at[leg, k],
                    recv_sem=recv.at[to_leg, k, me],
                    device_id={"section": section, "dp": 2 * lax.rem(y + dy, ny) + c},
                    device_id_type=MESH,
                ).start()

        if leg == 0:
            @pl.when(s < ns - 1)
            def _():
                send(s + 1, 0, (2, 1, 3, 0))

            @pl.when(s == ns - 1)
            def _():
                send(s, 1, (2, 1, 3))
                pltpu.make_async_copy(sbuf.at[0, k], u.at[1, k, me], recv.at[1, k, me]).start()
        else:
            @pl.when(s > 0)
            def _():
                send(s - 1, 1, (2, 1, 3, 0))

            owner = lax.div(k, per_owner)
            half = lax.rem(k, per_owner)

            @pl.when(owner == me)
            def _():
                pltpu.make_async_copy(
                    sbuf.at[1, k], obuf.at[half, me], own_recv.at[half, me]
                ).start()

            @pl.when(owner != me)
            def _():
                pltpu.make_async_remote_copy(
                    src_ref=sbuf.at[1, k],
                    dst_ref=obuf.at[half, me],
                    send_sem=own_send.at[k],
                    recv_sem=own_recv.at[half, me],
                    device_id={"section": s, "dp": owner},
                    device_id_type=MESH,
                ).start()

        wide_kap = jnp.concatenate([kap, kap], axis=1)
        for b in range(nb):
            value = u[leg, k, b][:, : 2 * hs].astype(f32) - wide_kap * xg[leg, k, b].astype(f32)
            xg[leg, k, b] = value.astype(jnp.bfloat16)

    lag = jnp.minimum(nc, LAG[0] + LAG[1] * (ns - 1 - s))

    def advance(i, _):
        @pl.when(i < nc)
        def _():
            step(0, i)

        @pl.when(i >= lag)
        def _():
            step(1, i - lag)

        return 0

    lax.fori_loop(0, nc + lag, advance, 0)

    stat_me[...] = jnp.zeros_like(stat_me)
    for leg in range(2):
        def tile(j, _, leg=leg):
            slot = lax.rem(j, 2)
            b = lax.div(j, 2)
            columns = pl.ds(pl.multiple_of(slot * nb * hs + b * hs, 128), hs)
            copy = pltpu.make_async_copy(
                gtile.at[slot], grads.at[1 - leg, 0, :, columns], tile_sem.at[slot]
            )

            @pl.when(j >= 2)
            def _():
                copy.wait()

            offset = pl.multiple_of(slot * hs, 128)
            right = xg[leg, :, b, :, pl.ds(offset, hs)].reshape(nc * T, hs)
            out = jnp.dot(h_t[leg], right, preferred_element_type=f32)
            gtile[slot] = out.astype(jnp.bfloat16)
            copy.start()
            folded = out.reshape(hs // 8, 8, hs)
            squares = jnp.sum(folded * folded, axis=0)
            tops = jnp.max(jnp.abs(folded), axis=0)
            for lane in range(0, hs, 128):
                stat_me[0] += squares[:, lane : lane + 128]
                stat_me[1] = jnp.maximum(stat_me[1], tops[:, lane : lane + 128])
            return 0

        lax.fori_loop(0, 2 * nb, tile, 0)
        for slot in range(2):
            pltpu.make_async_copy(
                gtile.at[slot], grads.at[1 - leg, 0, :, pl.ds(0, hs)], tile_sem.at[slot]
            ).wait()

    stat_dp[me] = stat_me[...]
    for j in range(1, nb):
        pltpu.make_async_remote_copy(
            src_ref=stat_me, dst_ref=stat_dp.at[me], send_sem=stat_send.at[0], recv_sem=stat_recv.at[0],
            device_id={"section": s, "dp": lax.rem(me + j, nb)}, device_id_type=MESH,
        ).start()
    some = stat_dp.at[pl.ds(0, nb - 1)]
    pltpu.make_async_copy(some, some, stat_recv.at[0]).wait()
    pltpu.make_async_copy(some, some, stat_send.at[0]).wait()
    both = stat_dp[...]
    stat_me[0] = jnp.sum(both[:, 0], axis=0)
    stat_me[1] = jnp.max(both[:, 1], axis=0)
    stat_sec[s] = stat_me[...]
    for j in range(1, ns):
        pltpu.make_async_remote_copy(
            src_ref=stat_me, dst_ref=stat_sec.at[s], send_sem=stat_send.at[1], recv_sem=stat_recv.at[1],
            device_id={"section": lax.rem(s + j, ns), "dp": me}, device_id_type=MESH,
        ).start()

    for half in range(per_owner):
        for b in range(nb):
            block = obuf.at[half, b]
            pltpu.make_async_copy(block, block, own_recv.at[half, b]).wait()
        kap = jnp.sum(obuf[half, :, :, 2 * hs :].astype(f32), axis=0)
        kap = jnp.concatenate([kap] * (hs // 128), axis=1)
        rows = pl.ds(half * T, T)
        for b in range(nb):
            for part in range(2):
                columns = pl.ds(part * nb * hs + b * hs, hs)
                value = obuf[half, b, :, part * hs : (part + 1) * hs].astype(f32)
                value -= kap * x_own[rows, columns].astype(f32)
                leaving[rows, columns] = value.astype(jnp.bfloat16)

    some = stat_sec.at[pl.ds(0, ns - 1)]
    pltpu.make_async_copy(some, some, stat_recv.at[1]).wait()
    pltpu.make_async_copy(some, some, stat_send.at[1]).wait()
    both = stat_sec[...]
    stats[0] = jnp.sum(both[:, 0], axis=0)
    stats[1] = jnp.max(both[:, 1], axis=0)

    def drain(k, _):
        four = u.at[0, k, pl.ds(0, ny)]
        three = u.at[0, k, pl.ds(0, ny - 1)]
        one = u.at[0, k, 0]

        @pl.when(s > 0)
        def _():
            pltpu.make_async_copy(four, four, relay_sem.at[0, k]).wait()
            pltpu.make_async_copy(four, four, send_sem.at[1, k]).wait()

        pltpu.make_async_copy(four, four, relay_sem.at[1, k]).wait()

        @pl.when(s < ns - 1)
        def _():
            pltpu.make_async_copy(four, four, send_sem.at[0, k]).wait()

        @pl.when(s == ns - 1)
        def _():
            pltpu.make_async_copy(three, three, send_sem.at[0, k]).wait()

        @pl.when(lax.div(k, per_owner) != me)
        def _():
            pltpu.make_async_copy(one, one, own_send.at[k]).wait()

        return 0

    lax.fori_loop(0, nc, drain, 0)


def passed_along(value, by):
    length = lax.axis_size("section")
    pairs = [(i, i + by) for i in range(length) if 0 <= i + by < length]
    return lax.ppermute(value, "section", pairs)


def on_device(cotangent, saved_inputs, weights):
    f32, bf16 = jnp.float32, jnp.bfloat16
    ns = lax.axis_size("section")
    nb = lax.axis_size("dp")
    s = lax.axis_index("section")
    hs, width = weights.shape[2:]
    rows = saved_inputs.shape[2] * saved_inputs.shape[3]
    per_owner = rows // T
    nc = per_owner * nb
    wide = 2 * hs + 128

    own = saved_inputs[:, 0].reshape(2, rows, width)[::-1]
    from_above = passed_along(own[0], 1)
    from_below = jnp.where(s == ns - 1, own[0], passed_along(own[1], -1))

    def blocked(value):
        legs = value.shape[0]
        value = value.reshape(legs, per_owner, T, 2, nb, hs)
        return value.transpose(0, 1, 4, 2, 3, 5).reshape(legs, per_owner, nb, T, 2 * hs)

    before = lax.all_gather(
        blocked(jnp.stack([from_above, from_below])), "dp", axis=1, tiled=True
    )
    start = blocked(cotangent.reshape(1, rows, width))[0]
    start = jnp.pad(start, ((0, 0), (0, 0), (0, 0), (0, 128)))
    start = lax.all_gather(start, "dp", axis=0, tiled=True)

    scale = lax.rsqrt(jnp.mean(jnp.square(own.astype(f32)), axis=-1) + epsilon)
    scale = lax.all_gather(scale, "dp", axis=1, tiled=True)[..., None]
    mine = lax.all_to_all(
        own.reshape(2, rows, 2, nb, hs), "dp", split_axis=3, concat_axis=1, tiled=True
    )[:, :, :, 0].astype(f32)
    first = mine[:, :, 0] * scale
    gate_in = mine[:, :, 1] * scale
    gated = jax.nn.sigmoid(gate_in)
    feats = first * gated
    coef = jnp.stack(
        [
            scale * gated,
            scale * feats * (1.0 - gated),
            scale * scale * feats * (1.0 + (1.0 - gated) * gate_in) / width,
        ],
        axis=1,
    ).reshape(2, 3, nc, T, hs)
    h_t = feats.astype(bf16).transpose(0, 2, 1)
    wt = weights[::-1, 0].reshape(2, hs, 2, nb, hs).transpose(0, 3, 2, 4, 1)
    wt = wt.reshape(2, nb, 2 * hs, hs)

    vmem = pl.BlockSpec(memory_space=pltpu.VMEM)
    hbm = pl.BlockSpec(memory_space=pl.ANY)
    dma = pltpu.SemaphoreType.DMA
    grads, leaving, stats = pl.pallas_call(
        functools.partial(relay_kernel, ns, nb, hs, nc),
        out_shape=(
            jax.ShapeDtypeStruct((2, 1, hs, width), bf16),
            jax.ShapeDtypeStruct((rows, width), bf16),
            jax.ShapeDtypeStruct((2, 8, 128), f32),
        ),
        in_specs=[hbm, hbm, hbm, vmem, vmem, vmem],
        out_specs=(hbm, vmem, vmem),
        scratch_shapes=[
            pltpu.VMEM((2, nb, 2 * hs, hs), bf16),
            pltpu.VMEM((2, nc, nb, T, 2 * hs), bf16),
            pltpu.VMEM((2, nc, nb, T, wide), bf16),
            pltpu.VMEM((2, nc, T, hs), f32),
            pltpu.VMEM((2, nc, T, wide), bf16),
            pltpu.VMEM((per_owner, nb, T, wide), bf16),
            pltpu.VMEM((2, hs, hs), bf16),
            pltpu.VMEM((nb, 2, 8, 128), f32),
            pltpu.VMEM((ns, 2, 8, 128), f32),
            pltpu.VMEM((2, 8, 128), f32),
            dma((2, nc, nb)),
            dma((2, nc)),
            dma((2, nc)),
            dma((nc,)),
            dma((per_owner, nb)),
            dma((2, 3)),
            dma((2,)),
            dma((2,)),
            dma((2,)),
        ],
        compiler_params=pltpu.CompilerParams(
            collective_id=0, has_side_effects=True, vmem_limit_bytes=58 * 2**20
        ),
        name="relay",
    )(wt, before, start, coef, h_t, own[1])

    total = jnp.sum(stats[0])
    largest = jnp.max(stats[1])
    limit = 0.5 * jnp.sqrt(jnp.float32(2 * ns * (width // 2) * width))
    factor = jnp.minimum(jnp.float32(1.0), limit / jnp.sqrt(total))
    weight_grads = (grads.astype(f32) * factor).astype(bf16)
    return (leaving.reshape(1, *cotangent.shape), weight_grads, factor * largest)


def solution(mesh):
    placed = (
        P(None, "dp", None),
        P(None, "section", None, "dp", None),
        P(None, "section", "dp", None),
    )
    return jax.shard_map(
        on_device,
        mesh=mesh,
        in_specs=placed,
        out_specs=(P("section", None, "dp", None), P(None, "section", "dp", None), P()),
        check_vma=False,
    )
```

```python
import functools

import jax
import jax.numpy as jnp
from jax import lax
from jax.experimental import pallas as pl
from jax.experimental.pallas import tpu as pltpu
from jax.sharding import PartitionSpec as P

epsilon = 1e-05
MESH = pl.DeviceIdType.MESH
T = 32
LAG = (3, 5)
QROWS = 256


def relay_kernel(
    ns, nb, hs, nc, w_hbm, x_hbm, cot_hbm,
    grads, leaving, stats,
    wt, xg, u, q, coef, feats, feats_t, sbuf, obuf, gtile, wpart, xrows, xs, rbuf,
    stat_dp, stat_sec, stat_me,
    recv, relay_sem, send_sem, own_send, own_recv, tile_sem, stat_send, stat_recv,
    w_sem, row_sem, xs_recv, xs_send, xs_own, r_recv, r_send, hop_send, x_recv, x_send,
):
    f32, bf16 = jnp.float32, jnp.bfloat16
    s = lax.axis_index("section")
    me = lax.axis_index("dp")
    y = lax.div(me, 2)
    c = lax.rem(me, 2)
    ny = nb // 2
    half_width = nb * hs
    partner = me + 1 - 2 * c
    per_owner = nc // nb
    rows = per_owner * T

    def at(section, dp):
        return {"section": section, "dp": dp}

    barrier = pltpu.get_barrier_semaphore()

    def greet(section, dp):
        pl.semaphore_signal(barrier, inc=1, device_id=at(section, dp), device_id_type=MESH)

    row_copy = pltpu.make_async_copy(x_hbm, xrows, row_sem)
    row_copy.start()

    for j in range(1, nb):
        greet(s, lax.rem(me + j, nb))
    for j in range(1, ns):
        greet(lax.rem(s + j, ns), me)

    @pl.when(s < ns - 1)
    def _():
        for j in range(ny):
            greet(s + 1, 2 * j + c)

    @pl.when(s > 0)
    def _():
        for j in range(ny):
            greet(s - 1, 2 * j + c)

    pl.semaphore_wait(
        barrier, nb - 1 + ns - 1 + ny * jnp.where(s < ns - 1, 1, 0) + ny * jnp.where(s > 0, 1, 0)
    )

    own_rows = pl.ds(per_owner * me, per_owner)

    def remote(src, dst, send, recv, section, dp):
        return pltpu.make_async_remote_copy(
            src_ref=src, dst_ref=dst, send_sem=send, recv_sem=recv,
            device_id=at(section, dp), device_id_type=MESH,
        )

    def send_slices(leg):
        for j in range(1, nb):
            dp = lax.rem(me + j, nb)
            for part in range(2):
                columns = pl.ds(pl.multiple_of(part * half_width + dp * hs, 128), hs)
                remote(
                    x_hbm.at[1 - leg, :, :, columns], xs.at[leg, me, :, :, pl.ds(part * hs, hs)],
                    xs_send.at[leg], xs_recv.at[leg], s, dp,
                ).start()
        for part in range(2):
            columns = pl.ds(pl.multiple_of(part * half_width + me * hs, 128), hs)
            pltpu.make_async_copy(
                x_hbm.at[1 - leg, :, :, columns], xs.at[leg, me, :, :, pl.ds(part * hs, hs)],
                xs_own.at[leg],
            ).start()

    def send_rows():
        @pl.when(s < ns - 1)
        def _():
            remote(
                x_hbm.at[1], xg.at[0, own_rows], hop_send.at[0], x_recv.at[0, me], s + 1, me
            ).start()

        @pl.when(s == 0)
        def _():
            pltpu.make_async_copy(cot_hbm, xg.at[0, own_rows], x_recv.at[0, me]).start()

        @pl.when(s > 0)
        def _():
            remote(
                x_hbm.at[0], xg.at[1, own_rows], hop_send.at[1], x_recv.at[1, me], s - 1, me
            ).start()

        @pl.when(s == ns - 1)
        def _():
            pltpu.make_async_copy(x_hbm.at[1], xg.at[1, own_rows], x_recv.at[1, me]).start()

    def send_scales(leg):
        total = jnp.zeros((per_owner, T, 128), f32)
        for lane in range(0, 2 * half_width, 128):
            value = xrows[1 - leg, :, :, lane : lane + 128].astype(f32)
            total += value * value
        mean = jnp.sum(total, axis=-1, keepdims=True) / (2 * half_width)
        rbuf[leg, me] = jnp.broadcast_to(lax.rsqrt(mean + epsilon), (per_owner, T, 128))
        for j in range(1, nb):
            remote(
                rbuf.at[leg, me], rbuf.at[leg, me], r_send.at[leg], r_recv.at[leg],
                s, lax.rem(me + j, nb),
            ).start()

    def rows_here(leg, owner):
        block = xg.at[leg, pl.ds(per_owner * owner, per_owner)]
        pltpu.make_async_copy(block, block, x_recv.at[leg, owner]).wait()
        return block

    def spread_rows(leg):
        block = rows_here(leg, me)
        for dy in (2, 1, 3):
            dp = 2 * lax.rem(y + dy, ny) + c
            remote(block, block, x_send.at[leg], x_recv.at[leg, me], s, dp).start()
        remote(block, block, x_send.at[leg], x_recv.at[leg, me], s, partner).start()

    def relay_rows(leg):
        for dy in (3, 1, 2):
            owner = 2 * lax.rem(y + dy, ny) + c
            block = rows_here(leg, owner)
            remote(block, block, x_send.at[leg], x_recv.at[leg, owner], s, partner).start()

    def transpose_weight(leg):
        def piece(j, slot):
            return pltpu.make_async_copy(
                w_hbm.at[1 - leg, 0, :, pl.ds(j * 2 * hs, 2 * hs)], wpart.at[slot], w_sem.at[slot]
            )

        piece(0, 0).start()
        for j in range(nb):
            slot = j % 2
            if j + 1 < nb:
                piece(j + 1, 1 - slot).start()
            piece(j, slot).wait()
            for i in range(2):
                column = 2 * j + i
                part, b = column // nb, column % nb
                wt[leg, b, part * hs : (part + 1) * hs, :] = wpart[slot, :, i * hs : (i + 1) * hs].T

    def local_factors(leg):
        some = xs.at[leg, pl.ds(0, nb - 1)]
        pltpu.make_async_copy(some, some, xs_recv.at[leg]).wait()
        one = xs.at[leg, 0]
        pltpu.make_async_copy(one, one, xs_own.at[leg]).wait()
        some = rbuf.at[leg, pl.ds(0, nb - 1)]
        pltpu.make_async_copy(some, some, r_recv.at[leg]).wait()

        def chunk(k, _):
            owner, half = lax.div(k, per_owner), lax.rem(k, per_owner)
            scale = jnp.concatenate([rbuf[leg, owner, half]] * (hs // 128), axis=1)
            value = xs[leg, owner, half].astype(f32)
            first = value[:, :hs] * scale
            gate_in = value[:, hs:] * scale
            gated = jax.nn.sigmoid(gate_in)
            feat = first * gated
            coef[leg, 0, k] = scale * gated
            coef[leg, 1, k] = scale * feat * (1.0 - gated)
            coef[leg, 2, k] = (
                scale * scale * feat * (1.0 + (1.0 - gated) * gate_in) / (2 * half_width)
            )
            feats[leg, k] = feat.astype(bf16)
            return 0

        lax.fori_loop(0, nc, chunk, 0)

    def columns_of(b, part):
        return pl.ds(part * half_width + b * hs, hs)

    def fill_q(leg):
        for dy in range(ny):
            rows_here(leg, 2 * lax.rem(y + dy, ny) + 1 - c)
        group = QROWS // T

        def fill(i, _):
            ks = pl.ds(i * group, group)
            total = jnp.zeros((QROWS, hs), f32)
            for b in range(nb):
                both = [xg[leg, ks, :, columns_of(b, part)].reshape(QROWS, hs) for part in range(2)]
                total += jnp.dot(
                    jnp.concatenate(both, axis=1), wt[leg, b], preferred_element_type=f32
                )
            q[leg, ks] = total.reshape(group, T, hs)
            return 0

        lax.fori_loop(0, nc // group, fill, 0)
        some = xg.at[leg, pl.ds(0, per_owner * (nb - 1))]
        pltpu.make_async_copy(some, some, x_send.at[leg]).wait()

    send_slices(0)
    send_rows()
    row_copy.wait()
    send_scales(0)
    spread_rows(0)
    send_slices(1)
    send_scales(1)

    @pl.when(s == 0)
    def _():
        def clear(k, _):
            for b in range(nb):
                u[0, k, b, :, : 2 * hs] = jnp.zeros((T, 2 * hs), bf16)
                u[0, k, b, :, 2 * hs :] = jnp.full((T, 128), -1.0 if b == 0 else 0.0, bf16)
            return 0

        lax.fori_loop(0, nc, clear, 0)

    transpose_weight(0)
    relay_rows(0)
    local_factors(0)
    fill_q(0)

    def step(leg, k):
        acc = jnp.zeros((T, hs), f32)

        def arrived(b):
            block = u.at[leg, k, b]
            pltpu.make_async_copy(block, block, recv.at[leg, k, b]).wait()

        for dy in (2, 3, 1, 0):
            b = 2 * lax.rem(y + dy, ny) + c

            def pass_on(b=b):
                arrived(b)
                pltpu.make_async_remote_copy(
                    src_ref=u.at[leg, k, b],
                    dst_ref=u.at[leg, k, b],
                    send_sem=relay_sem.at[leg, k],
                    recv_sem=recv.at[leg, k, b],
                    device_id={"section": s, "dp": partner},
                    device_id_type=MESH,
                ).start()

            if leg == 0:
                pl.when(s > 0)(pass_on)
            else:
                pass_on()
            acc += jnp.dot(u[leg, k, b][:, : 2 * hs], wt[leg, b], preferred_element_type=f32)
        for dy in (2, 3, 1, 0):
            b = 2 * lax.rem(y + dy, ny) + 1 - c
            if leg == 0:
                pl.when(s > 0)(functools.partial(arrived, b))
            else:
                arrived(b)
            acc += jnp.dot(u[leg, k, b][:, : 2 * hs], wt[leg, b], preferred_element_type=f32)
        kap = u[leg, k, 0][:, 2 * hs :].astype(f32)
        for b in range(1, nb):
            kap += u[leg, k, b][:, 2 * hs :].astype(f32)
        kap = jnp.concatenate([kap] * (hs // 128), axis=1)
        dh = acc - kap * q[leg, k]
        mine = u[leg, k, me].astype(f32)
        x_mine = [
            xg[leg, k, :, pl.ds(pl.multiple_of(part * half_width + me * hs, 128), hs)].astype(f32)
            for part in range(2)
        ]
        new_a = mine[:, :hs] - kap * x_mine[0] + coef[leg, 0, k] * dh
        new_g = mine[:, hs : 2 * hs] - kap * x_mine[1] + coef[leg, 1, k] * dh
        part = jnp.sum(coef[leg, 2, k] * dh, axis=1, keepdims=True)
        sbuf[leg, k, :, :hs] = new_a.astype(jnp.bfloat16)
        sbuf[leg, k, :, hs : 2 * hs] = new_g.astype(jnp.bfloat16)
        sbuf[leg, k, :, 2 * hs :] = jnp.broadcast_to(part, (T, 128)).astype(jnp.bfloat16)

        def send(section, to_leg, dys):
            for dy in dys:
                pltpu.make_async_remote_copy(
                    src_ref=sbuf.at[leg, k],
                    dst_ref=u.at[to_leg, k, me],
                    send_sem=send_sem.at[leg, k],
                    recv_sem=recv.at[to_leg, k, me],
                    device_id={"section": section, "dp": 2 * lax.rem(y + dy, ny) + c},
                    device_id_type=MESH,
                ).start()

        if leg == 0:
            @pl.when(s < ns - 1)
            def _():
                send(s + 1, 0, (2, 1, 3, 0))

            @pl.when(s == ns - 1)
            def _():
                send(s, 1, (2, 1, 3))
                pltpu.make_async_copy(sbuf.at[0, k], u.at[1, k, me], recv.at[1, k, me]).start()
        else:
            @pl.when(s > 0)
            def _():
                send(s - 1, 1, (2, 1, 3, 0))

            owner = lax.div(k, per_owner)
            half = lax.rem(k, per_owner)

            @pl.when(owner == me)
            def _():
                pltpu.make_async_copy(
                    sbuf.at[1, k], obuf.at[half, me], own_recv.at[half, me]
                ).start()

            @pl.when(owner != me)
            def _():
                pltpu.make_async_remote_copy(
                    src_ref=sbuf.at[1, k],
                    dst_ref=obuf.at[half, me],
                    send_sem=own_send.at[k],
                    recv_sem=own_recv.at[half, me],
                    device_id={"section": s, "dp": owner},
                    device_id_type=MESH,
                ).start()

        for b in range(nb):
            for part in range(2):
                value = u[leg, k, b, :, part * hs : (part + 1) * hs].astype(f32)
                value -= kap * xg[leg, k, :, columns_of(b, part)].astype(f32)
                xg[leg, k, :, columns_of(b, part)] = value.astype(bf16)

    def weight_grad(leg):
        feats_t[...] = feats[leg].reshape(nc * T, hs).T

        def tile(j, _):
            slot = lax.rem(j, 2)
            columns = pl.ds(pl.multiple_of(j * hs, 128), hs)
            copy = pltpu.make_async_copy(
                gtile.at[slot], grads.at[1 - leg, 0, :, columns], tile_sem.at[slot]
            )

            @pl.when(j >= 2)
            def _():
                copy.wait()

            right = xg[leg, :, :, columns].reshape(nc * T, hs)
            out = jnp.dot(feats_t[...], right, preferred_element_type=f32)
            gtile[slot] = out.astype(bf16)
            copy.start()
            folded = out.reshape(hs // 8, 8, hs)
            squares = jnp.sum(folded * folded, axis=0)
            tops = jnp.max(jnp.abs(folded), axis=0)
            for lane in range(0, hs, 128):
                stat_me[0] += squares[:, lane : lane + 128]
                stat_me[1] = jnp.maximum(stat_me[1], tops[:, lane : lane + 128])
            return 0

        lax.fori_loop(0, 2 * nb, tile, 0)
        for slot in range(2):
            pltpu.make_async_copy(
                gtile.at[slot], grads.at[1 - leg, 0, :, pl.ds(0, hs)], tile_sem.at[slot]
            ).wait()

    stat_me[...] = jnp.zeros_like(stat_me)
    lag = jnp.minimum(nc, LAG[0] + LAG[1] * (ns - 1 - s))
    early = lag < nc
    prepare_at = jnp.where(early, 0, nc)
    grad_at = jnp.where(early, nc + lag, nc)

    def advance(i, _):
        @pl.when(i == prepare_at)
        def _():
            spread_rows(1)
            relay_rows(1)
            transpose_weight(1)
            local_factors(1)
            fill_q(1)

        @pl.when(i == grad_at)
        def _():
            weight_grad(0)

        @pl.when(i < nc)
        def _():
            step(0, i)

        @pl.when((i >= lag) & (i < nc + lag))
        def _():
            step(1, i - lag)

        return 0

    lax.fori_loop(0, nc + lag + 1, advance, 0)
    weight_grad(1)

    stat_dp[me] = stat_me[...]
    for j in range(1, nb):
        pltpu.make_async_remote_copy(
            src_ref=stat_me, dst_ref=stat_dp.at[me], send_sem=stat_send.at[0], recv_sem=stat_recv.at[0],
            device_id={"section": s, "dp": lax.rem(me + j, nb)}, device_id_type=MESH,
        ).start()
    some = stat_dp.at[pl.ds(0, nb - 1)]
    pltpu.make_async_copy(some, some, stat_recv.at[0]).wait()
    pltpu.make_async_copy(some, some, stat_send.at[0]).wait()
    both = stat_dp[...]
    stat_me[0] = jnp.sum(both[:, 0], axis=0)
    stat_me[1] = jnp.max(both[:, 1], axis=0)
    stat_sec[s] = stat_me[...]
    for j in range(1, ns):
        pltpu.make_async_remote_copy(
            src_ref=stat_me, dst_ref=stat_sec.at[s], send_sem=stat_send.at[1], recv_sem=stat_recv.at[1],
            device_id={"section": lax.rem(s + j, ns), "dp": me}, device_id_type=MESH,
        ).start()

    for half in range(per_owner):
        for b in range(nb):
            block = obuf.at[half, b]
            pltpu.make_async_copy(block, block, own_recv.at[half, b]).wait()
        kap = jnp.sum(obuf[half, :, :, 2 * hs :].astype(f32), axis=0)
        kap = jnp.concatenate([kap] * (hs // 128), axis=1)
        for b in range(nb):
            for part in range(2):
                columns = columns_of(b, part)
                value = obuf[half, b, :, part * hs : (part + 1) * hs].astype(f32)
                value -= kap * xrows[0, half, :, columns].astype(f32)
                leaving[half, :, columns] = value.astype(bf16)

    some = stat_sec.at[pl.ds(0, ns - 1)]
    pltpu.make_async_copy(some, some, stat_recv.at[1]).wait()
    pltpu.make_async_copy(some, some, stat_send.at[1]).wait()
    both = stat_sec[...]
    stats[0] = jnp.sum(both[:, 0], axis=0)
    stats[1] = jnp.max(both[:, 1], axis=0)

    def drain(k, _):
        four = u.at[0, k, pl.ds(0, ny)]
        three = u.at[0, k, pl.ds(0, ny - 1)]
        one = u.at[0, k, 0]

        @pl.when(s > 0)
        def _():
            pltpu.make_async_copy(four, four, relay_sem.at[0, k]).wait()
            pltpu.make_async_copy(four, four, send_sem.at[1, k]).wait()

        pltpu.make_async_copy(four, four, relay_sem.at[1, k]).wait()

        @pl.when(s < ns - 1)
        def _():
            pltpu.make_async_copy(four, four, send_sem.at[0, k]).wait()

        @pl.when(s == ns - 1)
        def _():
            pltpu.make_async_copy(three, three, send_sem.at[0, k]).wait()

        @pl.when(lax.div(k, per_owner) != me)
        def _():
            pltpu.make_async_copy(one, one, own_send.at[k]).wait()

        return 0

    lax.fori_loop(0, nc, drain, 0)

    for leg in range(2):
        some = xs.at[leg, pl.ds(0, nb - 1)]
        pltpu.make_async_copy(some, some, xs_send.at[leg]).wait()
        some = rbuf.at[leg, pl.ds(0, nb - 1)]
        pltpu.make_async_copy(some, some, r_send.at[leg]).wait()
    one = xg.at[0, pl.ds(0, per_owner)]

    @pl.when(s < ns - 1)
    def _():
        pltpu.make_async_copy(one, one, hop_send.at[0]).wait()

    @pl.when(s > 0)
    def _():
        pltpu.make_async_copy(one, one, hop_send.at[1]).wait()


def on_device(cotangent, saved_inputs, weights):
    f32, bf16 = jnp.float32, jnp.bfloat16
    ns = lax.axis_size("section")
    nb = lax.axis_size("dp")
    hs, width = weights.shape[2:]
    rows = saved_inputs.shape[2] * saved_inputs.shape[3]
    per_owner = rows // T
    nc = per_owner * nb
    wide = 2 * hs + 128

    vmem = pl.BlockSpec(memory_space=pltpu.VMEM)
    hbm = pl.BlockSpec(memory_space=pl.ANY)
    dma = pltpu.SemaphoreType.DMA
    grads, leaving, stats = pl.pallas_call(
        functools.partial(relay_kernel, ns, nb, hs, nc),
        out_shape=(
            jax.ShapeDtypeStruct((2, 1, hs, width), bf16),
            jax.ShapeDtypeStruct((per_owner, T, width), bf16),
            jax.ShapeDtypeStruct((2, 8, 128), f32),
        ),
        in_specs=[hbm, hbm, hbm],
        out_specs=(hbm, vmem, vmem),
        scratch_shapes=[
            pltpu.VMEM((2, nb, 2 * hs, hs), bf16),
            pltpu.VMEM((2, nc, T, width), bf16),
            pltpu.VMEM((2, nc, nb, T, wide), bf16),
            pltpu.VMEM((2, nc, T, hs), f32),
            pltpu.VMEM((2, 3, nc, T, hs), f32),
            pltpu.VMEM((2, nc, T, hs), bf16),
            pltpu.VMEM((hs, nc * T), bf16),
            pltpu.VMEM((2, nc, T, wide), bf16),
            pltpu.VMEM((per_owner, nb, T, wide), bf16),
            pltpu.VMEM((2, hs, hs), bf16),
            pltpu.VMEM((2, hs, 2 * hs), bf16),
            pltpu.VMEM((2, per_owner, T, width), bf16),
            pltpu.VMEM((2, nb, per_owner, T, 2 * hs), bf16),
            pltpu.VMEM((2, nb, per_owner, T, 128), f32),
            pltpu.VMEM((nb, 2, 8, 128), f32),
            pltpu.VMEM((ns, 2, 8, 128), f32),
            pltpu.VMEM((2, 8, 128), f32),
            dma((2, nc, nb)),
            dma((2, nc)),
            dma((2, nc)),
            dma((nc,)),
            dma((per_owner, nb)),
            dma((2,)),
            dma((2,)),
            dma((2,)),
            dma((2,)),
            dma,
            dma((2,)),
            dma((2,)),
            dma((2,)),
            dma((2,)),
            dma((2,)),
            dma((2,)),
            dma((2, nb)),
            dma((2,)),
        ],
        compiler_params=pltpu.CompilerParams(
            collective_id=0, has_side_effects=True, vmem_limit_bytes=60 * 2**20
        ),
        name="relay",
    )(
        weights,
        saved_inputs.reshape(2, per_owner, T, width),
        cotangent.reshape(per_owner, T, width),
    )

    total = jnp.sum(stats[0])
    largest = jnp.max(stats[1])
    limit = 0.5 * jnp.sqrt(jnp.float32(2 * ns * (width // 2) * width))
    factor = jnp.minimum(jnp.float32(1.0), limit / jnp.sqrt(total))
    weight_grads = (grads.astype(f32) * factor).astype(bf16)
    return (leaving.reshape(1, *cotangent.shape), weight_grads, factor * largest)


def solution(mesh):
    placed = (
        P(None, "dp", None),
        P(None, "section", None, "dp", None),
        P(None, "section", "dp", None),
    )
    return jax.shard_map(
        on_device,
        mesh=mesh,
        in_specs=placed,
        out_specs=(P("section", None, "dp", None), P(None, "section", "dp", None), P()),
        check_vma=False,
    )
```

```python
import functools

import jax
import jax.numpy as jnp
from jax import lax
from jax.experimental import pallas as pl
from jax.experimental.pallas import tpu as pltpu
from jax.sharding import PartitionSpec as P

epsilon = 1e-05
MESH = pl.DeviceIdType.MESH
T = 16
TAKE = 1
LAG = (3, 7)
LAZY = 3
PREPARE = 9
GRAD = 4
DIRECT = (2, 0)


def relay_kernel(
    ns, nb, hs, nc, w_hbm, x_hbm, cot_hbm,
    grads, leaving, stats,
    wt, xg, u, q, coef, feats, feats_t, sbuf, obuf, gtile, wpart, xrows, xs, rbuf,
    stat_dp, stat_sec, stat_me,
    recv, relay_sem, send_sem, own_send, own_recv, tile_sem, stat_send, stat_recv,
    w_sem, row_sem, xs_recv, xs_send, xs_own, r_recv, r_send, hop_send, x_recv, x_send,
):
    f32, bf16 = jnp.float32, jnp.bfloat16
    s = lax.axis_index("section")
    me = lax.axis_index("dp")
    y = lax.div(me, 2)
    c = lax.rem(me, 2)
    ny = nb // 2
    half_width = nb * hs
    partner = me + 1 - 2 * c
    per_owner = nc // nb

    def at(section, dp):
        return {"section": section, "dp": dp}

    barrier = pltpu.get_barrier_semaphore()

    def greet(section, dp):
        pl.semaphore_signal(barrier, inc=1, device_id=at(section, dp), device_id_type=MESH)

    row_copy = pltpu.make_async_copy(x_hbm, xrows, row_sem)
    row_copy.start()

    for j in range(1, nb):
        greet(s, lax.rem(me + j, nb))
    for j in range(1, ns):
        greet(lax.rem(s + j, ns), me)

    @pl.when(s < ns - 1)
    def _():
        for j in range(ny):
            greet(s + 1, 2 * j + c)

    @pl.when(s > 0)
    def _():
        for j in range(ny):
            greet(s - 1, 2 * j + c)

    pl.semaphore_wait(
        barrier, nb - 1 + ns - 1 + ny * jnp.where(s < ns - 1, 1, 0) + ny * jnp.where(s > 0, 1, 0)
    )

    def remote(src, dst, send, recv, section, dp):
        return pltpu.make_async_remote_copy(
            src_ref=src, dst_ref=dst, send_sem=send, recv_sem=recv,
            device_id=at(section, dp), device_id_type=MESH,
        )

    def send_slices(leg):
        for j in range(1, nb):
            dp = lax.rem(me + j, nb)
            for part in range(2):
                columns = pl.ds(pl.multiple_of(part * half_width + dp * hs, 128), hs)
                remote(
                    x_hbm.at[1 - leg, :, :, columns], xs.at[leg, me, :, :, pl.ds(part * hs, hs)],
                    xs_send.at[leg], xs_recv.at[leg], s, dp,
                ).start()
        for part in range(2):
            columns = pl.ds(pl.multiple_of(part * half_width + me * hs, 128), hs)
            pltpu.make_async_copy(
                x_hbm.at[1 - leg, :, :, columns], xs.at[leg, me, :, :, pl.ds(part * hs, hs)],
                xs_own.at[leg],
            ).start()

    def send_rows(leg):
        for part in range(per_owner):
            own = xg.at[leg, part * nb + me]
            arrival = x_recv.at[leg, part, me]
            ends = (s < ns - 1, s == 0) if leg == 0 else (s > 0, s == ns - 1)

            @pl.when(ends[0])
            def _():
                remote(
                    x_hbm.at[1 - leg, part], own, hop_send.at[leg], arrival, s + 1 - 2 * leg, me
                ).start()

            @pl.when(ends[1])
            def _():
                first = cot_hbm.at[part] if leg == 0 else x_hbm.at[1, part]
                pltpu.make_async_copy(first, own, arrival).start()

    def send_scales(leg):
        total = jnp.zeros((per_owner, T, 128), f32)
        for lane in range(0, 2 * half_width, 128):
            value = xrows[1 - leg, :, :, lane : lane + 128].astype(f32)
            total += value * value
        mean = jnp.sum(total, axis=-1, keepdims=True) / (2 * half_width)
        rbuf[leg, me] = jnp.broadcast_to(lax.rsqrt(mean + epsilon), (per_owner, T, 128))
        for j in range(1, nb):
            remote(
                rbuf.at[leg, me], rbuf.at[leg, me], r_send.at[leg], r_recv.at[leg],
                s, lax.rem(me + j, nb),
            ).start()

    def rows_here(leg, part, owner):
        block = xg.at[leg, part * nb + owner]
        pltpu.make_async_copy(block, block, x_recv.at[leg, part, owner]).wait()
        return block

    def send_block(block, leg, part, owner, dp):
        remote(block, block, x_send.at[leg, part], x_recv.at[leg, part, owner], s, dp).start()

    def spread_rows(leg, part):
        block = rows_here(leg, part, me)
        for dy in (2, 1, 3):
            send_block(block, leg, part, me, 2 * lax.rem(y + dy, ny) + c)
        send_block(block, leg, part, me, partner)

    def relay_rows(leg, part):
        for dy in (3, 1, 2):
            owner = 2 * lax.rem(y + dy, ny) + c
            send_block(rows_here(leg, part, owner), leg, part, owner, partner)

    def transpose_weight(leg):
        def piece(j, slot):
            return pltpu.make_async_copy(
                w_hbm.at[1 - leg, 0, :, pl.ds(j * 2 * hs, 2 * hs)], wpart.at[slot], w_sem.at[slot]
            )

        piece(0, 0).start()
        for j in range(nb):
            slot = j % 2
            if j + 1 < nb:
                piece(j + 1, 1 - slot).start()
            piece(j, slot).wait()
            for i in range(2):
                column = 2 * j + i
                part, b = column // nb, column % nb
                wt[leg, b, part * hs : (part + 1) * hs, :] = wpart[slot, :, i * hs : (i + 1) * hs].T

    def local_factors(leg):
        some = xs.at[leg, pl.ds(0, nb - 1)]
        pltpu.make_async_copy(some, some, xs_recv.at[leg]).wait()
        one = xs.at[leg, 0]
        pltpu.make_async_copy(one, one, xs_own.at[leg]).wait()
        some = rbuf.at[leg, pl.ds(0, nb - 1)]
        pltpu.make_async_copy(some, some, r_recv.at[leg]).wait()

        def chunk(k, _):
            owner, half = lax.rem(k, nb), lax.div(k, nb)
            scale = jnp.concatenate([rbuf[leg, owner, half]] * (hs // 128), axis=1)
            value = xs[leg, owner, half].astype(f32)
            first = value[:, :hs] * scale
            gate_in = value[:, hs:] * scale
            gated = jax.nn.sigmoid(gate_in)
            feat = first * gated
            coef[leg, 0, k] = scale * gated
            coef[leg, 1, k] = scale * feat * (1.0 - gated)
            coef[leg, 2, k] = (
                scale * scale * feat * (1.0 + (1.0 - gated) * gate_in) / (2 * half_width)
            )
            feats[leg, k] = feat.astype(bf16)
            return 0

        lax.fori_loop(0, nc, chunk, 0)

    def columns_of(b, part):
        return pl.ds(part * half_width + b * hs, hs)

    def fill_q(leg, part):
        for dy in range(ny):
            rows_here(leg, part, 2 * lax.rem(y + dy, ny) + 1 - c)
        ks = pl.ds(part * nb, nb)
        total = jnp.zeros((nb * T, hs), f32)
        for b in range(nb):
            both = [xg[leg, ks, :, columns_of(b, i)].reshape(nb * T, hs) for i in range(2)]
            total += jnp.dot(
                jnp.concatenate(both, axis=1), wt[leg, b], preferred_element_type=f32
            )
        q[leg, ks] = total.reshape(nb, T, hs)
        some = xg.at[leg, pl.ds(0, nb - 1)]
        pltpu.make_async_copy(some, some, x_send.at[leg, part]).wait()

    send_slices(0)
    send_rows(0)
    row_copy.wait()
    send_scales(0)
    spread_rows(0, 0)

    @pl.when(s >= LAZY)
    def _():
        for part in range(1, per_owner):
            spread_rows(0, part)

    @pl.when(s == 0)
    def _():
        def clear(k, _):
            for b in range(nb):
                u[0, k, b, :, : 2 * hs] = jnp.zeros((T, 2 * hs), bf16)
                u[0, k, b, :, 2 * hs :] = jnp.full((T, 128), -1.0 if b == 0 else 0.0, bf16)
            return 0

        lax.fori_loop(0, nc, clear, 0)

    transpose_weight(0)
    relay_rows(0, 0)
    local_factors(0)
    fill_q(0, 0)

    @pl.when(s >= LAZY)
    def _():
        for part in range(1, per_owner):
            relay_rows(0, part)
            fill_q(0, part)

    def arrived(leg, k, b):
        block = u.at[leg, k, b]
        pltpu.make_async_copy(block, block, recv.at[leg, k, b]).wait()

    def pass_on(leg, k, b, dp):
        block = u.at[leg, k, b]
        remote(block, block, relay_sem.at[leg, k], recv.at[leg, k, b], s, dp).start()

    def lane_mate(dy):
        return 2 * lax.rem(y + dy, ny) + c

    def other_lane(dy):
        return lane_mate(dy) + 1 - 2 * c

    def blocks(leg, k, count, semaphore):
        some = u.at[leg, k, pl.ds(0, count)]
        pltpu.make_async_copy(some, some, semaphore).wait()

    def take(leg, k):
        arrived(leg, k, me)
        for dy in (1, 3):
            for mate in (lane_mate(dy), other_lane(dy)):
                pass_on(leg, k, me, mate)
        pass_on(leg, k, me, partner)

    def relay(leg, k):
        arrived(leg, k, lane_mate(2))
        pass_on(leg, k, lane_mate(2), partner)

    def sent(leg, k):
        if leg == 0:
            @pl.when(s < ns - 1)
            def _():
                blocks(leg, k, len(DIRECT), send_sem.at[leg, k])

            if len(DIRECT) > 1:
                @pl.when(s == ns - 1)
                def _():
                    blocks(leg, k, len(DIRECT) - 1, send_sem.at[leg, k])
        else:
            @pl.when(s > 0)
            def _():
                blocks(leg, k, len(DIRECT), send_sem.at[leg, k])

    def step(leg, k):
        acc = jnp.zeros((T, hs), f32)
        here = (lane_mate(0), lane_mate(2))
        due = (other_lane(0), lane_mate(3), other_lane(3), lane_mate(1), other_lane(1), other_lane(2))
        for n, b in enumerate(here + due):
            if n >= len(here):
                if leg == 0:
                    pl.when(s > 0)(functools.partial(arrived, leg, k, b))
                else:
                    arrived(leg, k, b)
            acc += jnp.dot(u[leg, k, b][:, : 2 * hs], wt[leg, b], preferred_element_type=f32)
        kap = u[leg, k, 0][:, 2 * hs :].astype(f32)
        for b in range(1, nb):
            kap += u[leg, k, b][:, 2 * hs :].astype(f32)
        kap = jnp.concatenate([kap] * (hs // 128), axis=1)
        dh = acc - kap * q[leg, k]
        mine = u[leg, k, me].astype(f32)
        x_mine = [
            xg[leg, k, :, pl.ds(pl.multiple_of(part * half_width + me * hs, 128), hs)].astype(f32)
            for part in range(2)
        ]
        new_a = mine[:, :hs] - kap * x_mine[0] + coef[leg, 0, k] * dh
        new_g = mine[:, hs : 2 * hs] - kap * x_mine[1] + coef[leg, 1, k] * dh
        part = jnp.sum(coef[leg, 2, k] * dh, axis=1, keepdims=True)
        sbuf[leg, k, :, :hs] = new_a.astype(jnp.bfloat16)
        sbuf[leg, k, :, hs : 2 * hs] = new_g.astype(jnp.bfloat16)
        sbuf[leg, k, :, 2 * hs :] = jnp.broadcast_to(part, (T, 128)).astype(jnp.bfloat16)

        @pl.when(k > 0)
        def _():
            sent(leg, k - 1)

        def send(section, to_leg, dys):
            for dy in dys:
                pltpu.make_async_remote_copy(
                    src_ref=sbuf.at[leg, k],
                    dst_ref=u.at[to_leg, k, me],
                    send_sem=send_sem.at[leg, k],
                    recv_sem=recv.at[to_leg, k, me],
                    device_id={"section": section, "dp": 2 * lax.rem(y + dy, ny) + c},
                    device_id_type=MESH,
                ).start()

        if leg == 0:
            @pl.when(s < ns - 1)
            def _():
                send(s + 1, 0, DIRECT)

            @pl.when(s == ns - 1)
            def _():
                send(s, 1, DIRECT[:-1])
                pltpu.make_async_copy(sbuf.at[0, k], u.at[1, k, me], recv.at[1, k, me]).start()
        else:
            @pl.when(s > 0)
            def _():
                send(s - 1, 1, DIRECT)

            owner = lax.rem(k, nb)
            half = lax.div(k, nb)

            @pl.when(owner == me)
            def _():
                pltpu.make_async_copy(
                    sbuf.at[1, k], obuf.at[half, me], own_recv.at[half, me]
                ).start()

            @pl.when(owner != me)
            def _():
                pltpu.make_async_remote_copy(
                    src_ref=sbuf.at[1, k],
                    dst_ref=obuf.at[half, me],
                    send_sem=own_send.at[k],
                    recv_sem=own_recv.at[half, me],
                    device_id={"section": s, "dp": owner},
                    device_id_type=MESH,
                ).start()

        for b in range(nb):
            for part in range(2):
                value = u[leg, k, b, :, part * hs : (part + 1) * hs].astype(f32)
                value -= kap * xg[leg, k, :, columns_of(b, part)].astype(f32)
                xg[leg, k, :, columns_of(b, part)] = value.astype(bf16)

    def weight_grad(leg):
        feats_t[...] = feats[leg].reshape(nc * T, hs).T

        def tile(j, _):
            slot = lax.rem(j, 2)
            columns = pl.ds(pl.multiple_of(j * hs, 128), hs)
            copy = pltpu.make_async_copy(
                gtile.at[slot], grads.at[1 - leg, 0, :, columns], tile_sem.at[slot]
            )

            @pl.when(j >= 2)
            def _():
                copy.wait()

            right = xg[leg, :, :, columns].reshape(nc * T, hs)
            out = jnp.dot(feats_t[...], right, preferred_element_type=f32)
            gtile[slot] = out.astype(bf16)
            copy.start()
            folded = out.reshape(hs // 8, 8, hs)
            squares = jnp.sum(folded * folded, axis=0)
            tops = jnp.max(jnp.abs(folded), axis=0)
            for lane in range(0, hs, 128):
                stat_me[0] += squares[:, lane : lane + 128]
                stat_me[1] = jnp.maximum(stat_me[1], tops[:, lane : lane + 128])
            return 0

        lax.fori_loop(0, 2 * nb, tile, 0)
        for slot in range(2):
            pltpu.make_async_copy(
                gtile.at[slot], grads.at[1 - leg, 0, :, pl.ds(0, hs)], tile_sem.at[slot]
            ).wait()

    stat_me[...] = jnp.zeros_like(stat_me)
    lag = jnp.minimum(nc - 1 + TAKE, LAG[0] + LAG[1] * (ns - 1 - s))
    grad_at = jnp.where(s < GRAD, nc - 1, nc + lag)

    def prepare():
        send_slices(1)
        send_rows(1)
        send_scales(1)
        for part in range(per_owner):
            spread_rows(1, part)
        for part in range(per_owner):
            relay_rows(1, part)
        transpose_weight(1)
        local_factors(1)
        for part in range(per_owner):
            fill_q(1, part)

    def advance(i, _):
        j = i - lag

        @pl.when((i == -TAKE) & (s >= PREPARE))
        def _():
            prepare()

        for ahead, action in ((nb + 1, spread_rows), (5, relay_rows), (2, fill_q)):
            k = i + ahead

            @pl.when((s < LAZY) & (k >= nb) & (k < nc) & (lax.rem(k, nb) == 0))
            def _(k=k, action=action):
                action(0, lax.div(k, nb))

        @pl.when((i + TAKE < nc) & (s > 0))
        def _():
            take(0, i + TAKE)

        @pl.when((i >= 0) & (i < nc))
        def _():
            step(0, i)

        @pl.when((i + TAKE < nc) & (s > 0))
        def _():
            relay(0, i + TAKE)

        @pl.when((i == nc - 1) & (s < PREPARE))
        def _():
            prepare()

        @pl.when(i == grad_at)
        def _():
            weight_grad(0)

        @pl.when((j + TAKE >= 0) & (j + TAKE < nc))
        def _():
            take(1, j + TAKE)

        @pl.when((j >= 0) & (j < nc))
        def _():
            step(1, j)

        @pl.when((j + TAKE >= 0) & (j + TAKE < nc))
        def _():
            relay(1, j + TAKE)

        return 0

    lax.fori_loop(-TAKE, nc + lag + 1, advance, 0)
    weight_grad(1)

    stat_dp[me] = stat_me[...]
    for j in range(1, nb):
        pltpu.make_async_remote_copy(
            src_ref=stat_me, dst_ref=stat_dp.at[me], send_sem=stat_send.at[0], recv_sem=stat_recv.at[0],
            device_id={"section": s, "dp": lax.rem(me + j, nb)}, device_id_type=MESH,
        ).start()
    some = stat_dp.at[pl.ds(0, nb - 1)]
    pltpu.make_async_copy(some, some, stat_recv.at[0]).wait()
    pltpu.make_async_copy(some, some, stat_send.at[0]).wait()
    both = stat_dp[...]
    stat_me[0] = jnp.sum(both[:, 0], axis=0)
    stat_me[1] = jnp.max(both[:, 1], axis=0)
    stat_sec[s] = stat_me[...]
    for j in range(1, ns):
        pltpu.make_async_remote_copy(
            src_ref=stat_me, dst_ref=stat_sec.at[s], send_sem=stat_send.at[1], recv_sem=stat_recv.at[1],
            device_id={"section": lax.rem(s + j, ns), "dp": me}, device_id_type=MESH,
        ).start()

    for half in range(per_owner):
        for b in range(nb):
            block = obuf.at[half, b]
            pltpu.make_async_copy(block, block, own_recv.at[half, b]).wait()
        kap = jnp.sum(obuf[half, :, :, 2 * hs :].astype(f32), axis=0)
        kap = jnp.concatenate([kap] * (hs // 128), axis=1)
        for b in range(nb):
            for part in range(2):
                columns = columns_of(b, part)
                value = obuf[half, b, :, part * hs : (part + 1) * hs].astype(f32)
                value -= kap * xrows[0, half, :, columns].astype(f32)
                leaving[half, :, columns] = value.astype(bf16)

    some = stat_sec.at[pl.ds(0, ns - 1)]
    pltpu.make_async_copy(some, some, stat_recv.at[1]).wait()
    pltpu.make_async_copy(some, some, stat_send.at[1]).wait()
    both = stat_sec[...]
    stats[0] = jnp.sum(both[:, 0], axis=0)
    stats[1] = jnp.max(both[:, 1], axis=0)

    sent(0, nc - 1)
    sent(1, nc - 1)

    def drain(k, _):
        one = u.at[0, k, 0]

        @pl.when(s > 0)
        def _():
            blocks(0, k, 6, relay_sem.at[0, k])

        blocks(1, k, 6, relay_sem.at[1, k])

        @pl.when(lax.rem(k, nb) != me)
        def _():
            pltpu.make_async_copy(one, one, own_send.at[k]).wait()

        return 0

    lax.fori_loop(0, nc, drain, 0)

    for leg in range(2):
        some = xs.at[leg, pl.ds(0, nb - 1)]
        pltpu.make_async_copy(some, some, xs_send.at[leg]).wait()
        some = rbuf.at[leg, pl.ds(0, nb - 1)]
        pltpu.make_async_copy(some, some, r_send.at[leg]).wait()
    one = xg.at[0, pl.ds(0, per_owner)]

    @pl.when(s < ns - 1)
    def _():
        pltpu.make_async_copy(one, one, hop_send.at[0]).wait()

    @pl.when(s > 0)
    def _():
        pltpu.make_async_copy(one, one, hop_send.at[1]).wait()


def on_device(cotangent, saved_inputs, weights):
    f32, bf16 = jnp.float32, jnp.bfloat16
    ns = lax.axis_size("section")
    nb = lax.axis_size("dp")
    hs, width = weights.shape[2:]
    rows = saved_inputs.shape[2] * saved_inputs.shape[3]
    per_owner = rows // T
    nc = per_owner * nb
    wide = 2 * hs + 128

    vmem = pl.BlockSpec(memory_space=pltpu.VMEM)
    hbm = pl.BlockSpec(memory_space=pl.ANY)
    dma = pltpu.SemaphoreType.DMA
    grads, leaving, stats = pl.pallas_call(
        functools.partial(relay_kernel, ns, nb, hs, nc),
        out_shape=(
            jax.ShapeDtypeStruct((2, 1, hs, width), bf16),
            jax.ShapeDtypeStruct((per_owner, T, width), bf16),
            jax.ShapeDtypeStruct((2, 8, 128), f32),
        ),
        in_specs=[hbm, hbm, hbm],
        out_specs=(hbm, vmem, vmem),
        scratch_shapes=[
            pltpu.VMEM((2, nb, 2 * hs, hs), bf16),
            pltpu.VMEM((2, nc, T, width), bf16),
            pltpu.VMEM((2, nc, nb, T, wide), bf16),
            pltpu.VMEM((2, nc, T, hs), f32),
            pltpu.VMEM((2, 3, nc, T, hs), f32),
            pltpu.VMEM((2, nc, T, hs), bf16),
            pltpu.VMEM((hs, nc * T), bf16),
            pltpu.VMEM((2, nc, T, wide), bf16),
            pltpu.VMEM((per_owner, nb, T, wide), bf16),
            pltpu.VMEM((2, hs, hs), bf16),
            pltpu.VMEM((2, hs, 2 * hs), bf16),
            pltpu.VMEM((2, per_owner, T, width), bf16),
            pltpu.VMEM((2, nb, per_owner, T, 2 * hs), bf16),
            pltpu.VMEM((2, nb, per_owner, T, 128), f32),
            pltpu.VMEM((nb, 2, 8, 128), f32),
            pltpu.VMEM((ns, 2, 8, 128), f32),
            pltpu.VMEM((2, 8, 128), f32),
            dma((2, nc, nb)),
            dma((2, nc)),
            dma((2, nc)),
            dma((nc,)),
            dma((per_owner, nb)),
            dma((2,)),
            dma((2,)),
            dma((2,)),
            dma((2,)),
            dma,
            dma((2,)),
            dma((2,)),
            dma((2,)),
            dma((2,)),
            dma((2,)),
            dma((2,)),
            dma((2, per_owner, nb)),
            dma((2, per_owner)),
        ],
        compiler_params=pltpu.CompilerParams(
            collective_id=0, has_side_effects=True, vmem_limit_bytes=60 * 2**20
        ),
        name="relay",
    )(
        weights,
        saved_inputs.reshape(2, per_owner, T, width),
        cotangent.reshape(per_owner, T, width),
    )

    total = jnp.sum(stats[0])
    largest = jnp.max(stats[1])
    limit = 0.5 * jnp.sqrt(jnp.float32(2 * ns * (width // 2) * width))
    factor = jnp.minimum(jnp.float32(1.0), limit / jnp.sqrt(total))
    weight_grads = (grads.astype(f32) * factor).astype(bf16)
    return (leaving.reshape(1, *cotangent.shape), weight_grads, factor * largest)


def solution(mesh):
    placed = (
        P(None, "dp", None),
        P(None, "section", None, "dp", None),
        P(None, "section", "dp", None),
    )
    return jax.shard_map(
        on_device,
        mesh=mesh,
        in_specs=placed,
        out_specs=(P("section", None, "dp", None), P(None, "section", "dp", None), P()),
        check_vma=False,
    )
```

```python
import functools

import jax
import jax.numpy as jnp
from jax import lax
from jax.experimental import pallas as pl
from jax.experimental.pallas import tpu as pltpu
from jax.sharding import PartitionSpec as P

epsilon = 1e-05
MESH = pl.DeviceIdType.MESH
T = 16
TAKE = 2
LAG = (4, 9)
LAZY = 3
PREPARE = 9
GRAD = 4
DIRECT = (0,)
FORWARD = (2, 1, 3)
PASS = 1


def relay_kernel(
    ns, nb, hs, nc, w_hbm, x_hbm, cot_hbm,
    grads, leaving, stats,
    wt, xg, u, q, coef, feats, feats_t, sbuf, obuf, gtile, wpart, xrows, xs, rbuf,
    stat_dp, stat_sec, stat_me,
    recv, relay_sem, send_sem, own_send, own_recv, tile_sem, stat_send, stat_recv,
    w_sem, row_sem, xs_recv, xs_send, xs_own, r_recv, r_send, hop_send, x_recv, x_send,
):
    f32, bf16 = jnp.float32, jnp.bfloat16
    s = lax.axis_index("section")
    me = lax.axis_index("dp")
    y = lax.div(me, 2)
    c = lax.rem(me, 2)
    ny = nb // 2
    half_width = nb * hs
    partner = me + 1 - 2 * c
    per_owner = nc // nb

    def at(section, dp):
        return {"section": section, "dp": dp}

    barrier = pltpu.get_barrier_semaphore()

    def greet(section, dp):
        pl.semaphore_signal(barrier, inc=1, device_id=at(section, dp), device_id_type=MESH)

    row_copy = pltpu.make_async_copy(x_hbm, xrows, row_sem)
    row_copy.start()

    for j in range(1, nb):
        greet(s, lax.rem(me + j, nb))
    for j in range(1, ns):
        greet(lax.rem(s + j, ns), me)

    @pl.when(s < ns - 1)
    def _():
        for j in range(ny):
            greet(s + 1, 2 * j + c)

    @pl.when(s > 0)
    def _():
        for j in range(ny):
            greet(s - 1, 2 * j + c)

    pl.semaphore_wait(
        barrier, nb - 1 + ns - 1 + ny * jnp.where(s < ns - 1, 1, 0) + ny * jnp.where(s > 0, 1, 0)
    )

    def remote(src, dst, send, recv, section, dp):
        return pltpu.make_async_remote_copy(
            src_ref=src, dst_ref=dst, send_sem=send, recv_sem=recv,
            device_id=at(section, dp), device_id_type=MESH,
        )

    def send_slices(leg):
        for j in range(1, nb):
            dp = lax.rem(me + j, nb)
            for part in range(2):
                columns = pl.ds(pl.multiple_of(part * half_width + dp * hs, 128), hs)
                remote(
                    x_hbm.at[1 - leg, :, :, columns], xs.at[leg, me, :, :, pl.ds(part * hs, hs)],
                    xs_send.at[leg], xs_recv.at[leg], s, dp,
                ).start()
        for part in range(2):
            columns = pl.ds(pl.multiple_of(part * half_width + me * hs, 128), hs)
            pltpu.make_async_copy(
                x_hbm.at[1 - leg, :, :, columns], xs.at[leg, me, :, :, pl.ds(part * hs, hs)],
                xs_own.at[leg],
            ).start()

    def send_rows(leg):
        for part in range(per_owner):
            own = xg.at[leg, part * nb + me]
            arrival = x_recv.at[leg, part, me]
            ends = (s < ns - 1, s == 0) if leg == 0 else (s > 0, s == ns - 1)

            @pl.when(ends[0])
            def _():
                remote(
                    x_hbm.at[1 - leg, part], own, hop_send.at[leg], arrival, s + 1 - 2 * leg, me
                ).start()

            @pl.when(ends[1])
            def _():
                first = cot_hbm.at[part] if leg == 0 else x_hbm.at[1, part]
                pltpu.make_async_copy(first, own, arrival).start()

    def send_scales(leg):
        total = jnp.zeros((per_owner, T, 128), f32)
        for lane in range(0, 2 * half_width, 128):
            value = xrows[1 - leg, :, :, lane : lane + 128].astype(f32)
            total += value * value
        mean = jnp.sum(total, axis=-1, keepdims=True) / (2 * half_width)
        rbuf[leg, me] = jnp.broadcast_to(lax.rsqrt(mean + epsilon), (per_owner, T, 128))
        for j in range(1, nb):
            remote(
                rbuf.at[leg, me], rbuf.at[leg, me], r_send.at[leg], r_recv.at[leg],
                s, lax.rem(me + j, nb),
            ).start()

    def rows_here(leg, part, owner):
        block = xg.at[leg, part * nb + owner]
        pltpu.make_async_copy(block, block, x_recv.at[leg, part, owner]).wait()
        return block

    def send_block(block, leg, part, owner, dp):
        remote(block, block, x_send.at[leg, part], x_recv.at[leg, part, owner], s, dp).start()

    def spread_rows(leg, part):
        block = rows_here(leg, part, me)
        for dy in (2, 1, 3):
            send_block(block, leg, part, me, 2 * lax.rem(y + dy, ny) + c)
        send_block(block, leg, part, me, partner)

    def relay_rows(leg, part):
        for dy in (3, 1, 2):
            owner = 2 * lax.rem(y + dy, ny) + c
            send_block(rows_here(leg, part, owner), leg, part, owner, partner)

    def transpose_weight(leg):
        def piece(j, slot):
            return pltpu.make_async_copy(
                w_hbm.at[1 - leg, 0, :, pl.ds(j * 2 * hs, 2 * hs)], wpart.at[slot], w_sem.at[slot]
            )

        piece(0, 0).start()
        for j in range(nb):
            slot = j % 2
            if j + 1 < nb:
                piece(j + 1, 1 - slot).start()
            piece(j, slot).wait()
            for i in range(2):
                column = 2 * j + i
                part, b = column // nb, column % nb
                wt[leg, b, part * hs : (part + 1) * hs, :] = wpart[slot, :, i * hs : (i + 1) * hs].T

    def local_factors(leg):
        some = xs.at[leg, pl.ds(0, nb - 1)]
        pltpu.make_async_copy(some, some, xs_recv.at[leg]).wait()
        one = xs.at[leg, 0]
        pltpu.make_async_copy(one, one, xs_own.at[leg]).wait()
        some = rbuf.at[leg, pl.ds(0, nb - 1)]
        pltpu.make_async_copy(some, some, r_recv.at[leg]).wait()

        def chunk(k, _):
            owner, half = lax.rem(k, nb), lax.div(k, nb)
            scale = jnp.concatenate([rbuf[leg, owner, half]] * (hs // 128), axis=1)
            value = xs[leg, owner, half].astype(f32)
            first = value[:, :hs] * scale
            gate_in = value[:, hs:] * scale
            gated = jax.nn.sigmoid(gate_in)
            feat = first * gated
            coef[leg, 0, k] = scale * gated
            coef[leg, 1, k] = scale * feat * (1.0 - gated)
            coef[leg, 2, k] = (
                scale * scale * feat * (1.0 + (1.0 - gated) * gate_in) / (2 * half_width)
            )
            feats[leg, k] = feat.astype(bf16)
            return 0

        lax.fori_loop(0, nc, chunk, 0)

    def columns_of(b, part):
        return pl.ds(part * half_width + b * hs, hs)

    def fill_q(leg, part):
        for dy in range(ny):
            rows_here(leg, part, 2 * lax.rem(y + dy, ny) + 1 - c)
        ks = pl.ds(part * nb, nb)
        total = jnp.zeros((nb * T, hs), f32)
        for b in range(nb):
            both = [xg[leg, ks, :, columns_of(b, i)].reshape(nb * T, hs) for i in range(2)]
            total += jnp.dot(
                jnp.concatenate(both, axis=1), wt[leg, b], preferred_element_type=f32
            )
        q[leg, ks] = total.reshape(nb, T, hs)
        some = xg.at[leg, pl.ds(0, nb - 1)]
        pltpu.make_async_copy(some, some, x_send.at[leg, part]).wait()

    send_slices(0)
    send_rows(0)
    row_copy.wait()
    send_scales(0)
    spread_rows(0, 0)

    @pl.when(s >= LAZY)
    def _():
        for part in range(1, per_owner):
            spread_rows(0, part)

    @pl.when(s == 0)
    def _():
        def clear(k, _):
            for b in range(nb):
                u[0, k, b % 2, b // 2, :, : 2 * hs] = jnp.zeros((T, 2 * hs), bf16)
                u[0, k, b % 2, b // 2, :, 2 * hs :] = jnp.full((T, 128), -1.0 if b == 0 else 0.0, bf16)
            return 0

        lax.fori_loop(0, nc, clear, 0)

    transpose_weight(0)
    relay_rows(0, 0)
    local_factors(0)
    fill_q(0, 0)

    @pl.when(s >= LAZY)
    def _():
        for part in range(1, per_owner):
            relay_rows(0, part)
            fill_q(0, part)

    def arrived(some, leg, k, which):
        pltpu.make_async_copy(some, some, recv.at[leg, k, which]).wait()

    def blocks(leg, k, count, semaphore):
        some = u.at[leg, k, 0, pl.ds(0, count)]
        pltpu.make_async_copy(some, some, semaphore).wait()

    def take(leg, k):
        block = u.at[leg, k, c, y]
        arrived(block, leg, k, 0)
        for dy in FORWARD:
            dp = 2 * lax.rem(y + dy, ny) + c
            remote(block, block, relay_sem.at[leg, k], recv.at[leg, k, 2], s, dp).start()

    def relay(leg, k):
        arrived(u.at[leg, k, 0, pl.ds(0, ny - 1)], leg, k, 2)
        lane_blocks = u.at[leg, k, c]
        remote(
            lane_blocks, lane_blocks, relay_sem.at[leg, k], recv.at[leg, k, 1], s, partner
        ).start()

    def sent(leg, k):
        if leg == 0:
            @pl.when(s < ns - 1)
            def _():
                blocks(leg, k, len(DIRECT), send_sem.at[leg, k])

            if len(DIRECT) > 1:
                @pl.when(s == ns - 1)
                def _():
                    blocks(leg, k, len(DIRECT) - 1, send_sem.at[leg, k])
        else:
            @pl.when(s > 0)
            def _():
                blocks(leg, k, len(DIRECT), send_sem.at[leg, k])

    def step(leg, k):
        acc = jnp.zeros((T, hs), f32)
        kap = jnp.zeros((T, 128), f32)
        for which, lane in enumerate((c, 1 - c)):
            if which == 1:
                all_four = functools.partial(arrived, u.at[leg, k, lane], leg, k, 1)
                if leg == 0:
                    pl.when(s > 0)(all_four)
                else:
                    all_four()
            for row in range(ny):
                block = u[leg, k, lane, row]
                acc += jnp.dot(
                    block[:, : 2 * hs], wt[leg, 2 * row + lane], preferred_element_type=f32
                )
                kap += block[:, 2 * hs :].astype(f32)
        kap = jnp.concatenate([kap] * (hs // 128), axis=1)
        dh = acc - kap * q[leg, k]
        mine = u[leg, k, c, y].astype(f32)
        x_mine = [
            xg[leg, k, :, pl.ds(pl.multiple_of(part * half_width + me * hs, 128), hs)].astype(f32)
            for part in range(2)
        ]
        new_a = mine[:, :hs] - kap * x_mine[0] + coef[leg, 0, k] * dh
        new_g = mine[:, hs : 2 * hs] - kap * x_mine[1] + coef[leg, 1, k] * dh
        part = jnp.sum(coef[leg, 2, k] * dh, axis=1, keepdims=True)
        sbuf[leg, k, :, :hs] = new_a.astype(jnp.bfloat16)
        sbuf[leg, k, :, hs : 2 * hs] = new_g.astype(jnp.bfloat16)
        sbuf[leg, k, :, 2 * hs :] = jnp.broadcast_to(part, (T, 128)).astype(jnp.bfloat16)

        def send(section, to_leg, dys):
            for dy in dys:
                pltpu.make_async_remote_copy(
                    src_ref=sbuf.at[leg, k],
                    dst_ref=u.at[to_leg, k, c, y],
                    send_sem=send_sem.at[leg, k],
                    recv_sem=recv.at[to_leg, k, 0 if dy == 0 else 2],
                    device_id={"section": section, "dp": 2 * lax.rem(y + dy, ny) + c},
                    device_id_type=MESH,
                ).start()

        if leg == 0:
            @pl.when(s < ns - 1)
            def _():
                send(s + 1, 0, DIRECT)

            @pl.when(s == ns - 1)
            def _():
                send(s, 1, DIRECT[:-1])
                pltpu.make_async_copy(sbuf.at[0, k], u.at[1, k, c, y], recv.at[1, k, 0]).start()
        else:
            @pl.when(s > 0)
            def _():
                send(s - 1, 1, DIRECT)

            owner = lax.rem(k, nb)
            half = lax.div(k, nb)

            @pl.when(owner == me)
            def _():
                pltpu.make_async_copy(
                    sbuf.at[1, k], obuf.at[half, me], own_recv.at[half, me]
                ).start()

            @pl.when(owner != me)
            def _():
                pltpu.make_async_remote_copy(
                    src_ref=sbuf.at[1, k],
                    dst_ref=obuf.at[half, me],
                    send_sem=own_send.at[k],
                    recv_sem=own_recv.at[half, me],
                    device_id={"section": s, "dp": owner},
                    device_id_type=MESH,
                ).start()

        for b in range(nb):
            for part in range(2):
                value = u[leg, k, b % 2, b // 2, :, part * hs : (part + 1) * hs].astype(f32)
                value -= kap * xg[leg, k, :, columns_of(b, part)].astype(f32)
                xg[leg, k, :, columns_of(b, part)] = value.astype(bf16)

    def weight_grad(leg):
        feats_t[...] = feats[leg].reshape(nc * T, hs).T

        def tile(j, _):
            slot = lax.rem(j, 2)
            columns = pl.ds(pl.multiple_of(j * hs, 128), hs)
            copy = pltpu.make_async_copy(
                gtile.at[slot], grads.at[1 - leg, 0, :, columns], tile_sem.at[slot]
            )

            @pl.when(j >= 2)
            def _():
                copy.wait()

            right = xg[leg, :, :, columns].reshape(nc * T, hs)
            out = jnp.dot(feats_t[...], right, preferred_element_type=f32)
            gtile[slot] = out.astype(bf16)
            copy.start()
            folded = out.reshape(hs // 8, 8, hs)
            squares = jnp.sum(folded * folded, axis=0)
            tops = jnp.max(jnp.abs(folded), axis=0)
            for lane in range(0, hs, 128):
                stat_me[0] += squares[:, lane : lane + 128]
                stat_me[1] = jnp.maximum(stat_me[1], tops[:, lane : lane + 128])
            return 0

        lax.fori_loop(0, 2 * nb, tile, 0)
        for slot in range(2):
            pltpu.make_async_copy(
                gtile.at[slot], grads.at[1 - leg, 0, :, pl.ds(0, hs)], tile_sem.at[slot]
            ).wait()

    stat_me[...] = jnp.zeros_like(stat_me)
    lag = jnp.minimum(nc - 1 + TAKE, LAG[0] + LAG[1] * (ns - 1 - s))
    grad_at = jnp.where(s < GRAD, nc - 1, nc + lag)

    def prepare():
        send_slices(1)
        send_rows(1)
        send_scales(1)
        for part in range(per_owner):
            spread_rows(1, part)
        for part in range(per_owner):
            relay_rows(1, part)
        transpose_weight(1)
        local_factors(1)
        for part in range(per_owner):
            fill_q(1, part)

    def advance(i, _):
        j = i - lag

        @pl.when((i == -TAKE) & (s >= PREPARE))
        def _():
            prepare()

        for ahead, action in ((nb + 1, spread_rows), (5, relay_rows), (2, fill_q)):
            k = i + ahead

            @pl.when((s < LAZY) & (k >= nb) & (k < nc) & (lax.rem(k, nb) == 0))
            def _(k=k, action=action):
                action(0, lax.div(k, nb))

        @pl.when((i + TAKE < nc) & (s > 0))
        def _():
            take(0, i + TAKE)

        @pl.when((i >= 0) & (i < nc))
        def _():
            if PASS == 0:
                pl.when(s > 0)(functools.partial(relay, 0, i))
            step(0, i)

        if PASS == 1:
            @pl.when((i + 1 >= 0) & (i + 1 < nc) & (s > 0))
            def _():
                relay(0, i + 1)

        @pl.when((i == nc - 1) & (s < PREPARE))
        def _():
            prepare()

        @pl.when(i == grad_at)
        def _():
            weight_grad(0)

        @pl.when((j + TAKE >= 0) & (j + TAKE < nc))
        def _():
            take(1, j + TAKE)

        @pl.when((j >= 0) & (j < nc))
        def _():
            if PASS == 0:
                relay(1, j)
            step(1, j)

        if PASS == 1:
            @pl.when((j + 1 >= 0) & (j + 1 < nc))
            def _():
                relay(1, j + 1)

        return 0

    lax.fori_loop(-TAKE, nc + lag + 1, advance, 0)
    weight_grad(1)

    stat_dp[me] = stat_me[...]
    for j in range(1, nb):
        pltpu.make_async_remote_copy(
            src_ref=stat_me, dst_ref=stat_dp.at[me], send_sem=stat_send.at[0], recv_sem=stat_recv.at[0],
            device_id={"section": s, "dp": lax.rem(me + j, nb)}, device_id_type=MESH,
        ).start()
    some = stat_dp.at[pl.ds(0, nb - 1)]
    pltpu.make_async_copy(some, some, stat_recv.at[0]).wait()
    pltpu.make_async_copy(some, some, stat_send.at[0]).wait()
    both = stat_dp[...]
    stat_me[0] = jnp.sum(both[:, 0], axis=0)
    stat_me[1] = jnp.max(both[:, 1], axis=0)
    stat_sec[s] = stat_me[...]
    for j in range(1, ns):
        pltpu.make_async_remote_copy(
            src_ref=stat_me, dst_ref=stat_sec.at[s], send_sem=stat_send.at[1], recv_sem=stat_recv.at[1],
            device_id={"section": lax.rem(s + j, ns), "dp": me}, device_id_type=MESH,
        ).start()

    for half in range(per_owner):
        for b in range(nb):
            block = obuf.at[half, b]
            pltpu.make_async_copy(block, block, own_recv.at[half, b]).wait()
        kap = jnp.sum(obuf[half, :, :, 2 * hs :].astype(f32), axis=0)
        kap = jnp.concatenate([kap] * (hs // 128), axis=1)
        for b in range(nb):
            for part in range(2):
                columns = columns_of(b, part)
                value = obuf[half, b, :, part * hs : (part + 1) * hs].astype(f32)
                value -= kap * xrows[0, half, :, columns].astype(f32)
                leaving[half, :, columns] = value.astype(bf16)

    some = stat_sec.at[pl.ds(0, ns - 1)]
    pltpu.make_async_copy(some, some, stat_recv.at[1]).wait()
    pltpu.make_async_copy(some, some, stat_send.at[1]).wait()
    both = stat_sec[...]
    stats[0] = jnp.sum(both[:, 0], axis=0)
    stats[1] = jnp.max(both[:, 1], axis=0)

    def drained(leg, k):
        some = obuf.at[0, pl.ds(0, ny + len(FORWARD))]
        pltpu.make_async_copy(some, some, relay_sem.at[leg, k]).wait()

    def drain(k, _):
        one = u.at[0, k, 0, 0]
        sent(0, k)
        sent(1, k)

        @pl.when(s > 0)
        def _():
            drained(0, k)

        drained(1, k)

        @pl.when(lax.rem(k, nb) != me)
        def _():
            pltpu.make_async_copy(one, one, own_send.at[k]).wait()

        return 0

    lax.fori_loop(0, nc, drain, 0)

    for leg in range(2):
        some = xs.at[leg, pl.ds(0, nb - 1)]
        pltpu.make_async_copy(some, some, xs_send.at[leg]).wait()
        some = rbuf.at[leg, pl.ds(0, nb - 1)]
        pltpu.make_async_copy(some, some, r_send.at[leg]).wait()
    one = xg.at[0, pl.ds(0, per_owner)]

    @pl.when(s < ns - 1)
    def _():
        pltpu.make_async_copy(one, one, hop_send.at[0]).wait()

    @pl.when(s > 0)
    def _():
        pltpu.make_async_copy(one, one, hop_send.at[1]).wait()


def scale_kernel(factor, grads, scaled):
    scaled[...] = (grads[...].astype(jnp.float32) * factor[0]).astype(jnp.bfloat16)


def on_device(cotangent, saved_inputs, weights):
    f32, bf16 = jnp.float32, jnp.bfloat16
    ns = lax.axis_size("section")
    nb = lax.axis_size("dp")
    hs, width = weights.shape[2:]
    rows = saved_inputs.shape[2] * saved_inputs.shape[3]
    per_owner = rows // T
    nc = per_owner * nb
    wide = 2 * hs + 128
    ny = nb // 2

    vmem = pl.BlockSpec(memory_space=pltpu.VMEM)
    hbm = pl.BlockSpec(memory_space=pl.ANY)
    dma = pltpu.SemaphoreType.DMA
    grads, leaving, stats = pl.pallas_call(
        functools.partial(relay_kernel, ns, nb, hs, nc),
        out_shape=(
            jax.ShapeDtypeStruct((2, 1, hs, width), bf16),
            jax.ShapeDtypeStruct((per_owner, T, width), bf16),
            jax.ShapeDtypeStruct((2, 8, 128), f32),
        ),
        in_specs=[hbm, hbm, hbm],
        out_specs=(hbm, vmem, vmem),
        scratch_shapes=[
            pltpu.VMEM((2, nb, 2 * hs, hs), bf16),
            pltpu.VMEM((2, nc, T, width), bf16),
            pltpu.VMEM((2, nc, 2, ny, T, wide), bf16),
            pltpu.VMEM((2, nc, T, hs), f32),
            pltpu.VMEM((2, 3, nc, T, hs), f32),
            pltpu.VMEM((2, nc, T, hs), bf16),
            pltpu.VMEM((hs, nc * T), bf16),
            pltpu.VMEM((2, nc, T, wide), bf16),
            pltpu.VMEM((per_owner, nb, T, wide), bf16),
            pltpu.VMEM((2, hs, hs), bf16),
            pltpu.VMEM((2, hs, 2 * hs), bf16),
            pltpu.VMEM((2, per_owner, T, width), bf16),
            pltpu.VMEM((2, nb, per_owner, T, 2 * hs), bf16),
            pltpu.VMEM((2, nb, per_owner, T, 128), f32),
            pltpu.VMEM((nb, 2, 8, 128), f32),
            pltpu.VMEM((ns, 2, 8, 128), f32),
            pltpu.VMEM((2, 8, 128), f32),
            dma((2, nc, 3)),
            dma((2, nc)),
            dma((2, nc)),
            dma((nc,)),
            dma((per_owner, nb)),
            dma((2,)),
            dma((2,)),
            dma((2,)),
            dma((2,)),
            dma,
            dma((2,)),
            dma((2,)),
            dma((2,)),
            dma((2,)),
            dma((2,)),
            dma((2,)),
            dma((2, per_owner, nb)),
            dma((2, per_owner)),
        ],
        compiler_params=pltpu.CompilerParams(
            collective_id=0, has_side_effects=True, vmem_limit_bytes=60 * 2**20
        ),
        name="relay",
    )(
        weights,
        saved_inputs.reshape(2, per_owner, T, width),
        cotangent.reshape(per_owner, T, width),
    )

    total = jnp.sum(stats[0])
    largest = jnp.max(stats[1])
    limit = 0.5 * jnp.sqrt(jnp.float32(2 * ns * (width // 2) * width))
    factor = jnp.minimum(jnp.float32(1.0), limit / jnp.sqrt(total))
    piece = pl.BlockSpec((1, 1, hs // 6, width), lambda leg, i: (leg, 0, i, 0))
    weight_grads = pl.pallas_call(
        scale_kernel,
        grid=(2, 6),
        out_shape=jax.ShapeDtypeStruct(grads.shape, bf16),
        in_specs=[pl.BlockSpec(memory_space=pltpu.SMEM), piece],
        out_specs=piece,
        name="scale",
    )(factor.reshape(1), grads)
    return (leaving.reshape(1, *cotangent.shape), weight_grads, factor * largest)


def solution(mesh):
    placed = (
        P(None, "dp", None),
        P(None, "section", None, "dp", None),
        P(None, "section", "dp", None),
    )
    return jax.shard_map(
        on_device,
        mesh=mesh,
        in_specs=placed,
        out_specs=(P("section", None, "dp", None), P(None, "section", "dp", None), P()),
        check_vma=False,
    )
```

```python
import functools

import jax
import jax.numpy as jnp
from jax import lax
from jax.experimental import pallas as pl
from jax.experimental.pallas import tpu as pltpu
from jax.sharding import PartitionSpec as P

epsilon = 1e-05
MESH = pl.DeviceIdType.MESH
T = 16
TAKE = 2
LAG = (4, 9)
LAZY = 3
PREPARE = 10
AHEAD = 8
GRAD = 4
DIRECT = (0,)
FORWARD = (2, 1, 3)
PASS = 1


def relay_kernel(
    ns, nb, hs, nc, w_hbm, x_hbm, cot_hbm,
    grads, leaving, stats,
    wt, xg, u, q, coef, feats, feats_t, sbuf, obuf, gtile, wpart, xrows, xs, rbuf,
    stat_dp, stat_sec, stat_me,
    recv, relay_sem, send_sem, own_send, own_recv, tile_sem, stat_send, stat_recv,
    w_sem, row_sem, xs_recv, xs_send, xs_own, r_recv, r_send, hop_send, x_recv, x_send,
):
    f32, bf16 = jnp.float32, jnp.bfloat16
    s = lax.axis_index("section")
    me = lax.axis_index("dp")
    y = lax.div(me, 2)
    c = lax.rem(me, 2)
    ny = nb // 2
    half_width = nb * hs
    partner = me + 1 - 2 * c
    per_owner = nc // nb

    def at(section, dp):
        return {"section": section, "dp": dp}

    barrier = pltpu.get_barrier_semaphore()

    def greet(section, dp):
        pl.semaphore_signal(barrier, inc=1, device_id=at(section, dp), device_id_type=MESH)

    row_copy = pltpu.make_async_copy(x_hbm, xrows, row_sem)
    row_copy.start()

    for j in range(1, nb):
        greet(s, lax.rem(me + j, nb))
    for j in range(1, ns):
        greet(lax.rem(s + j, ns), me)

    @pl.when(s < ns - 1)
    def _():
        for j in range(ny):
            greet(s + 1, 2 * j + c)

    @pl.when(s > 0)
    def _():
        for j in range(ny):
            greet(s - 1, 2 * j + c)

    pl.semaphore_wait(
        barrier, nb - 1 + ns - 1 + ny * jnp.where(s < ns - 1, 1, 0) + ny * jnp.where(s > 0, 1, 0)
    )

    def remote(src, dst, send, recv, section, dp):
        return pltpu.make_async_remote_copy(
            src_ref=src, dst_ref=dst, send_sem=send, recv_sem=recv,
            device_id=at(section, dp), device_id_type=MESH,
        )

    def send_slices(leg):
        for j in range(1, nb):
            dp = lax.rem(me + j, nb)
            for part in range(2):
                columns = pl.ds(pl.multiple_of(part * half_width + dp * hs, 128), hs)
                remote(
                    x_hbm.at[1 - leg, :, :, columns], xs.at[leg, me, :, :, pl.ds(part * hs, hs)],
                    xs_send.at[leg], xs_recv.at[leg], s, dp,
                ).start()
        for part in range(2):
            columns = pl.ds(pl.multiple_of(part * half_width + me * hs, 128), hs)
            pltpu.make_async_copy(
                x_hbm.at[1 - leg, :, :, columns], xs.at[leg, me, :, :, pl.ds(part * hs, hs)],
                xs_own.at[leg],
            ).start()

    def send_rows(leg):
        for part in range(per_owner):
            own = xg.at[leg, part * nb + me]
            arrival = x_recv.at[leg, part, me]
            ends = (s < ns - 1, s == 0) if leg == 0 else (s > 0, s == ns - 1)

            @pl.when(ends[0])
            def _():
                remote(
                    x_hbm.at[1 - leg, part], own, hop_send.at[leg], arrival, s + 1 - 2 * leg, me
                ).start()

            @pl.when(ends[1])
            def _():
                first = cot_hbm.at[part] if leg == 0 else x_hbm.at[1, part]
                pltpu.make_async_copy(first, own, arrival).start()

    def send_scales(leg):
        total = jnp.zeros((per_owner, T, 128), f32)
        for lane in range(0, 2 * half_width, 128):
            value = xrows[1 - leg, :, :, lane : lane + 128].astype(f32)
            total += value * value
        mean = jnp.sum(total, axis=-1, keepdims=True) / (2 * half_width)
        rbuf[leg, me] = jnp.broadcast_to(lax.rsqrt(mean + epsilon), (per_owner, T, 128))
        for j in range(1, nb):
            remote(
                rbuf.at[leg, me], rbuf.at[leg, me], r_send.at[leg], r_recv.at[leg],
                s, lax.rem(me + j, nb),
            ).start()

    def rows_here(leg, part, owner):
        block = xg.at[leg, part * nb + owner]
        pltpu.make_async_copy(block, block, x_recv.at[leg, part, owner]).wait()
        return block

    def send_block(block, leg, part, owner, dp):
        remote(block, block, x_send.at[leg, part], x_recv.at[leg, part, owner], s, dp).start()

    def spread_rows(leg, part):
        block = rows_here(leg, part, me)
        for dy in (2, 1, 3):
            send_block(block, leg, part, me, 2 * lax.rem(y + dy, ny) + c)
        send_block(block, leg, part, me, partner)

    def relay_rows(leg, part):
        for dy in (3, 1, 2):
            owner = 2 * lax.rem(y + dy, ny) + c
            send_block(rows_here(leg, part, owner), leg, part, owner, partner)

    def transpose_weight(leg):
        def piece(j, slot):
            return pltpu.make_async_copy(
                w_hbm.at[1 - leg, 0, :, pl.ds(j * 2 * hs, 2 * hs)], wpart.at[slot], w_sem.at[slot]
            )

        piece(0, 0).start()
        for j in range(nb):
            slot = j % 2
            if j + 1 < nb:
                piece(j + 1, 1 - slot).start()
            piece(j, slot).wait()
            for i in range(2):
                column = 2 * j + i
                part, b = column // nb, column % nb
                wt[leg, b, part * hs : (part + 1) * hs, :] = wpart[slot, :, i * hs : (i + 1) * hs].T

    def local_factors(leg):
        some = xs.at[leg, pl.ds(0, nb - 1)]
        pltpu.make_async_copy(some, some, xs_recv.at[leg]).wait()
        one = xs.at[leg, 0]
        pltpu.make_async_copy(one, one, xs_own.at[leg]).wait()
        some = rbuf.at[leg, pl.ds(0, nb - 1)]
        pltpu.make_async_copy(some, some, r_recv.at[leg]).wait()

        def chunk(k, _):
            owner, half = lax.rem(k, nb), lax.div(k, nb)
            scale = jnp.concatenate([rbuf[leg, owner, half]] * (hs // 128), axis=1)
            value = xs[leg, owner, half].astype(f32)
            first = value[:, :hs] * scale
            gate_in = value[:, hs:] * scale
            gated = jax.nn.sigmoid(gate_in)
            feat = first * gated
            coef[leg, 0, k] = scale * gated
            coef[leg, 1, k] = scale * feat * (1.0 - gated)
            coef[leg, 2, k] = (
                scale * scale * feat * (1.0 + (1.0 - gated) * gate_in) / (2 * half_width)
            )
            feats[leg, k] = feat.astype(bf16)
            return 0

        lax.fori_loop(0, nc, chunk, 0)

    def columns_of(b, part):
        return pl.ds(part * half_width + b * hs, hs)

    def fill_q(leg, part):
        for dy in range(ny):
            rows_here(leg, part, 2 * lax.rem(y + dy, ny) + 1 - c)
        ks = pl.ds(part * nb, nb)
        total = jnp.zeros((nb * T, hs), f32)
        for b in range(nb):
            both = [xg[leg, ks, :, columns_of(b, i)].reshape(nb * T, hs) for i in range(2)]
            total += jnp.dot(
                jnp.concatenate(both, axis=1), wt[leg, b], preferred_element_type=f32
            )
        q[leg, ks] = total.reshape(nb, T, hs)
        some = xg.at[leg, pl.ds(0, nb - 1)]
        pltpu.make_async_copy(some, some, x_send.at[leg, part]).wait()

    send_slices(0)
    send_rows(0)
    row_copy.wait()
    send_scales(0)
    spread_rows(0, 0)

    @pl.when(s >= LAZY)
    def _():
        for part in range(1, per_owner):
            spread_rows(0, part)

    @pl.when(s == 0)
    def _():
        def clear(k, _):
            for b in range(nb):
                u[0, k, b % 2, b // 2, :, : 2 * hs] = jnp.zeros((T, 2 * hs), bf16)
                u[0, k, b % 2, b // 2, :, 2 * hs :] = jnp.full((T, 128), -1.0 if b == 0 else 0.0, bf16)
            return 0

        lax.fori_loop(0, nc, clear, 0)

    transpose_weight(0)
    relay_rows(0, 0)
    local_factors(0)
    fill_q(0, 0)

    @pl.when(s >= LAZY)
    def _():
        for part in range(1, per_owner):
            relay_rows(0, part)
            fill_q(0, part)

    def arrived(some, leg, k, which):
        pltpu.make_async_copy(some, some, recv.at[leg, k, which]).wait()

    def blocks(leg, k, count, semaphore):
        some = u.at[leg, k, 0, pl.ds(0, count)]
        pltpu.make_async_copy(some, some, semaphore).wait()

    def take(leg, k):
        block = u.at[leg, k, c, y]
        arrived(block, leg, k, 0)
        for dy in FORWARD:
            dp = 2 * lax.rem(y + dy, ny) + c
            remote(block, block, relay_sem.at[leg, k], recv.at[leg, k, 2], s, dp).start()

    def relay(leg, k):
        arrived(u.at[leg, k, 0, pl.ds(0, ny - 1)], leg, k, 2)
        lane_blocks = u.at[leg, k, c]
        remote(
            lane_blocks, lane_blocks, relay_sem.at[leg, k], recv.at[leg, k, 1], s, partner
        ).start()

    def sent(leg, k):
        if leg == 0:
            @pl.when(s < ns - 1)
            def _():
                blocks(leg, k, len(DIRECT), send_sem.at[leg, k])

            if len(DIRECT) > 1:
                @pl.when(s == ns - 1)
                def _():
                    blocks(leg, k, len(DIRECT) - 1, send_sem.at[leg, k])
        else:
            @pl.when(s > 0)
            def _():
                blocks(leg, k, len(DIRECT), send_sem.at[leg, k])

    def step(leg, k):
        acc = jnp.zeros((T, hs), f32)
        kap = jnp.zeros((T, 128), f32)
        for which, lane in enumerate((c, 1 - c)):
            if which == 1:
                all_four = functools.partial(arrived, u.at[leg, k, lane], leg, k, 1)
                if leg == 0:
                    pl.when(s > 0)(all_four)
                else:
                    all_four()
            for row in range(ny):
                block = u[leg, k, lane, row]
                acc += jnp.dot(
                    block[:, : 2 * hs], wt[leg, 2 * row + lane], preferred_element_type=f32
                )
                kap += block[:, 2 * hs :].astype(f32)
        kap = jnp.concatenate([kap] * (hs // 128), axis=1)
        dh = acc - kap * q[leg, k]
        mine = u[leg, k, c, y].astype(f32)
        x_mine = [
            xg[leg, k, :, pl.ds(pl.multiple_of(part * half_width + me * hs, 128), hs)].astype(f32)
            for part in range(2)
        ]
        new_a = mine[:, :hs] - kap * x_mine[0] + coef[leg, 0, k] * dh
        new_g = mine[:, hs : 2 * hs] - kap * x_mine[1] + coef[leg, 1, k] * dh
        part = jnp.sum(coef[leg, 2, k] * dh, axis=1, keepdims=True)
        sbuf[leg, k, :, :hs] = new_a.astype(jnp.bfloat16)
        sbuf[leg, k, :, hs : 2 * hs] = new_g.astype(jnp.bfloat16)
        sbuf[leg, k, :, 2 * hs :] = jnp.broadcast_to(part, (T, 128)).astype(jnp.bfloat16)

        def send(section, to_leg, dys):
            for dy in dys:
                pltpu.make_async_remote_copy(
                    src_ref=sbuf.at[leg, k],
                    dst_ref=u.at[to_leg, k, c, y],
                    send_sem=send_sem.at[leg, k],
                    recv_sem=recv.at[to_leg, k, 0 if dy == 0 else 2],
                    device_id={"section": section, "dp": 2 * lax.rem(y + dy, ny) + c},
                    device_id_type=MESH,
                ).start()

        if leg == 0:
            @pl.when(s < ns - 1)
            def _():
                send(s + 1, 0, DIRECT)

            @pl.when(s == ns - 1)
            def _():
                send(s, 1, DIRECT[:-1])
                pltpu.make_async_copy(sbuf.at[0, k], u.at[1, k, c, y], recv.at[1, k, 0]).start()
        else:
            @pl.when(s > 0)
            def _():
                send(s - 1, 1, DIRECT)

            owner = lax.rem(k, nb)
            half = lax.div(k, nb)

            @pl.when(owner == me)
            def _():
                pltpu.make_async_copy(
                    sbuf.at[1, k], obuf.at[half, me], own_recv.at[half, me]
                ).start()

            @pl.when(owner != me)
            def _():
                pltpu.make_async_remote_copy(
                    src_ref=sbuf.at[1, k],
                    dst_ref=obuf.at[half, me],
                    send_sem=own_send.at[k],
                    recv_sem=own_recv.at[half, me],
                    device_id={"section": s, "dp": owner},
                    device_id_type=MESH,
                ).start()

        for b in range(nb):
            for part in range(2):
                value = u[leg, k, b % 2, b // 2, :, part * hs : (part + 1) * hs].astype(f32)
                value -= kap * xg[leg, k, :, columns_of(b, part)].astype(f32)
                xg[leg, k, :, columns_of(b, part)] = value.astype(bf16)

    def weight_grad(leg):
        feats_t[...] = feats[leg].reshape(nc * T, hs).T

        def tile(j, _):
            slot = lax.rem(j, 2)
            columns = pl.ds(pl.multiple_of(j * hs, 128), hs)
            copy = pltpu.make_async_copy(
                gtile.at[slot], grads.at[1 - leg, 0, :, columns], tile_sem.at[slot]
            )

            @pl.when(j >= 2)
            def _():
                copy.wait()

            right = xg[leg, :, :, columns].reshape(nc * T, hs)
            out = jnp.dot(feats_t[...], right, preferred_element_type=f32)
            gtile[slot] = out.astype(bf16)
            copy.start()
            folded = out.reshape(hs // 8, 8, hs)
            squares = jnp.sum(folded * folded, axis=0)
            tops = jnp.max(jnp.abs(folded), axis=0)
            for lane in range(0, hs, 128):
                stat_me[0] += squares[:, lane : lane + 128]
                stat_me[1] = jnp.maximum(stat_me[1], tops[:, lane : lane + 128])
            return 0

        lax.fori_loop(0, 2 * nb, tile, 0)
        for slot in range(2):
            pltpu.make_async_copy(
                gtile.at[slot], grads.at[1 - leg, 0, :, pl.ds(0, hs)], tile_sem.at[slot]
            ).wait()

    stat_me[...] = jnp.zeros_like(stat_me)
    lag = jnp.minimum(nc - 1 + TAKE, LAG[0] + LAG[1] * (ns - 1 - s))
    grad_at = jnp.where(s < GRAD, nc - 1, nc + lag)

    def fetch():
        send_slices(1)
        send_rows(1)
        send_scales(1)

    def spread():
        for part in range(per_owner):
            spread_rows(1, part)

    def prepare():
        @pl.when((s < AHEAD) | (s >= PREPARE))
        def _():
            fetch()
            spread()

        for part in range(per_owner):
            relay_rows(1, part)
        transpose_weight(1)
        local_factors(1)
        for part in range(per_owner):
            fill_q(1, part)

    def advance(i, _):
        j = i - lag

        @pl.when((i == -TAKE) & (s >= PREPARE))
        def _():
            prepare()

        for ahead, action in ((nb + 1, spread_rows), (5, relay_rows), (2, fill_q)):
            k = i + ahead

            @pl.when((s < LAZY) & (k >= nb) & (k < nc) & (lax.rem(k, nb) == 0))
            def _(k=k, action=action):
                action(0, lax.div(k, nb))

        @pl.when((i + TAKE < nc) & (s > 0))
        def _():
            take(0, i + TAKE)

        @pl.when((i >= 0) & (i < nc))
        def _():
            if PASS == 0:
                pl.when(s > 0)(functools.partial(relay, 0, i))
            step(0, i)

        if PASS == 1:
            @pl.when((i + 1 >= 0) & (i + 1 < nc) & (s > 0))
            def _():
                relay(0, i + 1)

        between = (s >= AHEAD) & (s < PREPARE)
        pl.when((i == nc // 4) & between)(fetch)
        pl.when((i == nc - nc // 4) & between)(spread)

        @pl.when((i == nc - 1) & (s < PREPARE))
        def _():
            prepare()

        @pl.when(i == grad_at)
        def _():
            weight_grad(0)

        @pl.when((j + TAKE >= 0) & (j + TAKE < nc))
        def _():
            take(1, j + TAKE)

        @pl.when((j >= 0) & (j < nc))
        def _():
            if PASS == 0:
                relay(1, j)
            step(1, j)

        if PASS == 1:
            @pl.when((j + 1 >= 0) & (j + 1 < nc))
            def _():
                relay(1, j + 1)

        return 0

    lax.fori_loop(-TAKE, nc + lag + 1, advance, 0)
    weight_grad(1)

    stat_dp[me] = stat_me[...]
    for j in range(1, nb):
        pltpu.make_async_remote_copy(
            src_ref=stat_me, dst_ref=stat_dp.at[me], send_sem=stat_send.at[0], recv_sem=stat_recv.at[0],
            device_id={"section": s, "dp": lax.rem(me + j, nb)}, device_id_type=MESH,
        ).start()
    some = stat_dp.at[pl.ds(0, nb - 1)]
    pltpu.make_async_copy(some, some, stat_recv.at[0]).wait()
    pltpu.make_async_copy(some, some, stat_send.at[0]).wait()
    both = stat_dp[...]
    stat_me[0] = jnp.sum(both[:, 0], axis=0)
    stat_me[1] = jnp.max(both[:, 1], axis=0)
    stat_sec[s] = stat_me[...]
    for j in range(1, ns):
        pltpu.make_async_remote_copy(
            src_ref=stat_me, dst_ref=stat_sec.at[s], send_sem=stat_send.at[1], recv_sem=stat_recv.at[1],
            device_id={"section": lax.rem(s + j, ns), "dp": me}, device_id_type=MESH,
        ).start()

    for half in range(per_owner):
        for b in range(nb):
            block = obuf.at[half, b]
            pltpu.make_async_copy(block, block, own_recv.at[half, b]).wait()
        kap = jnp.sum(obuf[half, :, :, 2 * hs :].astype(f32), axis=0)
        kap = jnp.concatenate([kap] * (hs // 128), axis=1)
        for b in range(nb):
            for part in range(2):
                columns = columns_of(b, part)
                value = obuf[half, b, :, part * hs : (part + 1) * hs].astype(f32)
                value -= kap * xrows[0, half, :, columns].astype(f32)
                leaving[half, :, columns] = value.astype(bf16)

    some = stat_sec.at[pl.ds(0, ns - 1)]
    pltpu.make_async_copy(some, some, stat_recv.at[1]).wait()
    pltpu.make_async_copy(some, some, stat_send.at[1]).wait()
    both = stat_sec[...]
    stats[0] = jnp.sum(both[:, 0], axis=0)
    stats[1] = jnp.max(both[:, 1], axis=0)

    def drained(leg, k):
        some = obuf.at[0, pl.ds(0, ny + len(FORWARD))]
        pltpu.make_async_copy(some, some, relay_sem.at[leg, k]).wait()

    def drain(k, _):
        one = u.at[0, k, 0, 0]
        sent(0, k)
        sent(1, k)

        @pl.when(s > 0)
        def _():
            drained(0, k)

        drained(1, k)

        @pl.when(lax.rem(k, nb) != me)
        def _():
            pltpu.make_async_copy(one, one, own_send.at[k]).wait()

        return 0

    lax.fori_loop(0, nc, drain, 0)

    for leg in range(2):
        some = xs.at[leg, pl.ds(0, nb - 1)]
        pltpu.make_async_copy(some, some, xs_send.at[leg]).wait()
        some = rbuf.at[leg, pl.ds(0, nb - 1)]
        pltpu.make_async_copy(some, some, r_send.at[leg]).wait()
    one = xg.at[0, pl.ds(0, per_owner)]

    @pl.when(s < ns - 1)
    def _():
        pltpu.make_async_copy(one, one, hop_send.at[0]).wait()

    @pl.when(s > 0)
    def _():
        pltpu.make_async_copy(one, one, hop_send.at[1]).wait()


def on_device(cotangent, saved_inputs, weights):
    f32, bf16 = jnp.float32, jnp.bfloat16
    ns = lax.axis_size("section")
    nb = lax.axis_size("dp")
    hs, width = weights.shape[2:]
    rows = saved_inputs.shape[2] * saved_inputs.shape[3]
    per_owner = rows // T
    nc = per_owner * nb
    wide = 2 * hs + 128
    ny = nb // 2

    vmem = pl.BlockSpec(memory_space=pltpu.VMEM)
    hbm = pl.BlockSpec(memory_space=pl.ANY)
    dma = pltpu.SemaphoreType.DMA
    grads, leaving, stats = pl.pallas_call(
        functools.partial(relay_kernel, ns, nb, hs, nc),
        out_shape=(
            jax.ShapeDtypeStruct((2, 1, hs, width), bf16),
            jax.ShapeDtypeStruct((per_owner, T, width), bf16),
            jax.ShapeDtypeStruct((2, 8, 128), f32),
        ),
        in_specs=[hbm, hbm, hbm],
        out_specs=(hbm, vmem, vmem),
        scratch_shapes=[
            pltpu.VMEM((2, nb, 2 * hs, hs), bf16),
            pltpu.VMEM((2, nc, T, width), bf16),
            pltpu.VMEM((2, nc, 2, ny, T, wide), bf16),
            pltpu.VMEM((2, nc, T, hs), f32),
            pltpu.VMEM((2, 3, nc, T, hs), f32),
            pltpu.VMEM((2, nc, T, hs), bf16),
            pltpu.VMEM((hs, nc * T), bf16),
            pltpu.VMEM((2, nc, T, wide), bf16),
            pltpu.VMEM((per_owner, nb, T, wide), bf16),
            pltpu.VMEM((2, hs, hs), bf16),
            pltpu.VMEM((2, hs, 2 * hs), bf16),
            pltpu.VMEM((2, per_owner, T, width), bf16),
            pltpu.VMEM((2, nb, per_owner, T, 2 * hs), bf16),
            pltpu.VMEM((2, nb, per_owner, T, 128), f32),
            pltpu.VMEM((nb, 2, 8, 128), f32),
            pltpu.VMEM((ns, 2, 8, 128), f32),
            pltpu.VMEM((2, 8, 128), f32),
            dma((2, nc, 3)),
            dma((2, nc)),
            dma((2, nc)),
            dma((nc,)),
            dma((per_owner, nb)),
            dma((2,)),
            dma((2,)),
            dma((2,)),
            dma((2,)),
            dma,
            dma((2,)),
            dma((2,)),
            dma((2,)),
            dma((2,)),
            dma((2,)),
            dma((2,)),
            dma((2, per_owner, nb)),
            dma((2, per_owner)),
        ],
        compiler_params=pltpu.CompilerParams(
            collective_id=0, has_side_effects=True, vmem_limit_bytes=60 * 2**20
        ),
        name="relay",
    )(
        weights,
        saved_inputs.reshape(2, per_owner, T, width),
        cotangent.reshape(per_owner, T, width),
    )

    total = jnp.sum(stats[0])
    largest = jnp.max(stats[1])
    limit = 0.5 * jnp.sqrt(jnp.float32(2 * ns * (width // 2) * width))
    factor = jnp.minimum(jnp.float32(1.0), limit / jnp.sqrt(total))
    weight_grads = (grads.astype(f32) * factor).astype(bf16)
    return (leaving.reshape(1, *cotangent.shape), weight_grads, factor * largest)


def solution(mesh):
    placed = (
        P(None, "dp", None),
        P(None, "section", None, "dp", None),
        P(None, "section", "dp", None),
    )
    return jax.shard_map(
        on_device,
        mesh=mesh,
        in_specs=placed,
        out_specs=(P("section", None, "dp", None), P(None, "section", "dp", None), P()),
        check_vma=False,
    )
```
